128 devices in a mesh: side: 2 (over core), dev: 64 (over x, y, z).
Axes of the slice: x: 4, y: 4, z: 4, core: 2. Of those that a mesh axis runs over, the one named last changes fastest.
Arguments:
- queries: bfloat16 [1024, 64, 576], P(('side', 'dev')), may hold values from -6 to 6
- latent_cache: bfloat16 [1024, 1024, 576], P(('side', 'dev')), may hold values from -6 to 6
- cache_lengths: int32 [1024], P(('side', 'dev')), may hold values from 256 to 1024, as said below
- residual: bfloat16 [1024, 7168], P('side', 'dev'), may hold values from -6 to 6
- value_up: bfloat16 [64, 512, 128], P('dev'), may hold values from -0.25 to 0.25
- out_proj: bfloat16 [8192, 7168], P(None, 'dev'), may hold values from -0.0625 to 0.0625
- norm_gain: bfloat16 [7168], P('dev'), may hold values from 0.25 to 1.75
- expert_ids: int32 [1024, 8], P('side'), may hold values from 0 to 255, all different within a row; in each aligned block of 512 rows (0 to 511, 512 to 1023, ...) at most 32 rows name the same one
- route_weights: float32 [1024, 8], P('side'), may hold values from 0.3 to 3
- w_gate: bfloat16 [7168, 32768], P(None, ('side', 'dev')), may hold values from -0.0625 to 0.0625
- w_up: bfloat16 [7168, 32768], P(None, ('side', 'dev')), may hold values from -0.0625 to 0.0625
- w_down: bfloat16 [32768, 7168], P(('side', 'dev')), may hold values from -0.1875 to 0.1875
Outputs:
- layer_out: bfloat16 [1024, 7168], P('side', 'dev')
The draws below stay inside these ranges and needn't reach their ends.
Inputs may be any that keep to these rules, and one draw needn't show every extreme that they name: `expert_ids`: among the 512 requests of one group no expert is named by more than 32 of them, and one expert is named by exactly 32; a row names 8 different experts. `cache_lengths`: request 0 has all 1024 positions valid.
All inputs are finite; a program needn't handle non-finite values.
Results may differ from the reference program's by a relative error of at most 0.007.
Values may be sent and summed in bfloat16 or wider, within the bound.
A program may use at most 128 MiB of HBM per device.

```python
import math
import jax
import jax.numpy as jnp
import numpy as np
from jax import lax

D = 7168
LATENT = 512
ROPE = 64
VDIM = 128
EXPERTS = 256
TOP = 8
HEADS = 64
HID = 1024
LEN = 1024
REQS = 1024
GROUP = 512
EXP_W = 32
CAP = 32
N_SIDE = 2


def shared_parts(key, strength):
    width = LATENT + ROPE
    keys = jax.random.split(key, 7)
    signs = jnp.where(jax.random.bernoulli(keys[0], 0.5, (REQS, width)), 1.0, -1.0).astype(jnp.float32)
    forced = jax.random.randint(keys[1], (), 0, REQS, dtype=jnp.int32)
    is_forced = jnp.arange(REQS, dtype=jnp.int32) == forced
    picked = (jax.random.uniform(keys[2], (REQS,)) < 0.125) | is_forced
    picked = picked & (strength > 0)
    key_level = 2.0 + 0.25 * jax.random.randint(keys[3], (REQS,), 0, 3, dtype=jnp.int32).astype(jnp.float32)
    key_level = strength * jnp.where(is_forced, 2.5, key_level)
    head_level = 1.5 + 0.25 * jax.random.randint(keys[4], (HEADS,), 0, 9, dtype=jnp.int32).astype(jnp.float32)
    head_level = strength * head_level.at[HEADS - 1].set(3.5)
    head_pick = (jax.random.uniform(keys[5], (REQS, HEADS)) < 0.25) | (jnp.arange(HEADS) == HEADS - 1)[None, :]
    step = max(1, LEN // 8)
    first = jax.random.randint(keys[6], (REQS,), 0, step, dtype=jnp.int32)
    return (signs, picked, key_level, head_level, head_pick, first, step)


def draw_queries(key, part):
    own = jax.random.fold_in(key, 21)
    shape = (REQS, HEADS, LATENT + ROPE)
    base = jnp.clip(jax.random.normal(own, shape, jnp.float32), -6.0, 6.0)
    strength = 0.0
    signs, picked, key_level, head_level, head_pick, first, step = shared_parts(key, strength)
    aligned = head_level[None, :, None] * signs[:, None, :]
    chosen = picked[:, None] & head_pick
    return jnp.where(chosen[:, :, None], aligned, base).astype(jnp.bfloat16)


def draw_latent_cache(key, part):
    own = jax.random.fold_in(key, 23)
    width = LATENT + ROPE
    shape = (REQS, LEN, width)
    base = jnp.clip(jax.random.normal(own, shape, jnp.float32), -6.0, 6.0)
    strength = 0.0
    signs, picked, key_level, head_level, head_pick, first, step = shared_parts(key, strength)
    rows = jnp.arange(REQS, dtype=jnp.int32)
    alternate = jnp.where(jnp.arange(width) % 2 == 0, 1.0, -1.0).astype(jnp.float32)
    top_row = key_level[:, None] * signs
    lower_level = key_level
    second_row = signs * (lower_level[:, None] + 1.25 * strength * alternate[None, :])
    second = first + step
    base = base.at[rows, first].set(jnp.where(picked[:, None], top_row, base[rows, first]))
    base = base.at[rows, second].set(jnp.where(picked[:, None], second_row, base[rows, second]))
    return base.astype(jnp.bfloat16)


def draw_cache_lengths(key, part):
    key = jax.random.fold_in(key, 11)
    drawn = jax.random.randint(key, (REQS,), LEN // 4, LEN + 1, dtype=jnp.int32)
    drawn = drawn.at[0].set(LEN)
    return drawn.at[1].set(LEN // 4)


def block_levels(stream_key, dims, cuts, smallest, top_value):
    loudness, own = 1.0, jax.random.fold_in(stream_key, 6)
    for axis_at, parts in cuts:
        heights = jnp.exp(jax.random.uniform(jax.random.fold_in(own, axis_at), (parts,), jnp.float32, smallest / len(cuts), top_value / len(cuts)))
        loudness = loudness * jnp.repeat(heights, dims[axis_at] // parts).reshape([-1 if axis == axis_at else 1 for axis in range(len(dims))])
    return loudness


def assign_block(stream_key, own, number, rows, amount, top, bound, slope):
    sequence = jax.random.permutation(stream_key, amount)
    packed, common = load_shares(amount, rows * top, bound, slope, True), load_shares(amount, rows * top, bound, slope, False)
    places = jnp.arange(amount)

    def named(tallies, rotation):
        used = int((tallies > 0).sum())
        fixed = max(1, used // 4)
        passed = fixed + (places - fixed + rotation * (used - fixed)) % max(1, amount - fixed)
        return jnp.zeros((amount,), jnp.int32).at[sequence[jnp.where(places < fixed, places, passed)]].set(jnp.asarray(tallies, jnp.int32))

    tallies = jnp.where(number % 4 == 0, named(packed, number // 4), named(common, number - number // 4 - 1))
    mixed = jax.random.permutation(jax.random.fold_in(own, 3), amount)
    giver, receiver = mixed[0:amount // 2 * 2:2], mixed[1:amount // 2 * 2:2]
    slack = jnp.minimum(tallies[giver] - 1, bound - tallies[receiver]) // 2
    slack = jnp.where((giver == sequence[0]) | (receiver == sequence[0]) | (tallies[receiver] == 0), 0, jnp.maximum(slack, 0))
    passed = jax.random.randint(jax.random.fold_in(own, 4), (amount // 2,), 0, 1 << 20) % (slack + 1)
    tallies = tallies.at[giver].add(-passed).at[receiver].add(passed)
    members = jnp.searchsorted(jnp.cumsum(tallies), jnp.arange(rows * top), side="right").astype(jnp.int32)
    listing = members.reshape(top, rows).T
    listing = listing[jax.random.permutation(jax.random.fold_in(own, 1), rows)]
    rotation = jax.random.randint(jax.random.fold_in(own, 2), (rows, 1), 0, top)
    return jnp.take_along_axis(listing, (jnp.arange(top)[None, :] + rotation) % top, axis=1)


def load_shares(number_of, total, reach, skew, full):
    weights = [(1 << 20) // math.isqrt(standing ** skew) + 1 for standing in range(1, number_of + 1)]
    largest = reach if full else min(reach, max(-(-total // number_of), total * weights[0] // sum(weights)))
    least = 1 if total - largest >= number_of - 1 else 0
    counts, surplus = [largest] + [least] * (number_of - 1), total - largest - least * (number_of - 1)
    while surplus > 0:
        movable = [i for i in range(1, number_of) if counts[i] < largest] or [i for i in range(1, number_of) if counts[i] < reach]
        mass, budget = sum([weights[i] for i in movable]), surplus
        for i in movable:
            more = min(reach - counts[i], max(1, budget * weights[i] // mass), surplus)
            counts[i] = counts[i] + more
            surplus = surplus - more
    return np.array(counts)


def bell_draw(own_key, extent, scale, most, cuts=(), held_as=jnp.bfloat16):
    entries = jax.random.normal(own_key, extent, jnp.float32) * scale
    if len(cuts) > 0:
        entries = block_levels(own_key, extent, cuts, -0.22, 0.18) * entries
    return jnp.clip(entries, min=-most, max=most).astype(held_as)


def setup_inputs(seed: int = 0) -> dict:
    streams_of = jax.random.split(jax.random.key(seed), 13)
    queries = draw_queries(jax.random.fold_in(streams_of[12], 71), 0)
    latent_cache = draw_latent_cache(jax.random.fold_in(streams_of[12], 71), 0)
    cache_lengths = draw_cache_lengths(jax.random.fold_in(streams_of[12], 71), 0)
    residual = bell_draw(streams_of[3], (REQS, D), 1.0, 6.0, ((0, 2), (1, 64)))
    value_up = bell_draw(streams_of[4], (HEADS, LATENT, VDIM), LATENT ** -0.5, 0.25, ((0, 64),))
    out_proj = bell_draw(streams_of[5], (HEADS * VDIM, D), (HEADS * VDIM) ** -0.5, 0.0625, ((1, 64),))
    norm_gain = jnp.clip(1.0 + 0.15 * jax.random.normal(streams_of[6], (D,), jnp.float32), 0.25, 1.75).astype(jnp.bfloat16)
    expert_ids_keys = jax.random.split(jax.random.fold_in(streams_of[7], 1), REQS // GROUP)
    expert_ids_turns = jax.random.permutation(jax.random.fold_in(streams_of[7], 3), REQS // GROUP)
    expert_ids = jax.vmap(lambda own, number: assign_block(jax.random.fold_in(streams_of[7], 2), own, number, GROUP, EXPERTS, TOP, CAP, 2))(expert_ids_keys, expert_ids_turns).reshape((REQS, TOP))
    route_weights = jnp.clip(jnp.exp(math.log(3.0) - 2.3025851 * jax.random.uniform(streams_of[8], (REQS, TOP), jnp.float32) ** block_levels(streams_of[8], (REQS, TOP), ((0, 2),), -0.2, 0.2)), 0.3, 3.0)
    w_gate = bell_draw(streams_of[9], (D, EXP_W * HID), D ** -0.5, 0.0625, ((1, 128),))
    w_up = bell_draw(streams_of[10], (D, EXP_W * HID), D ** -0.5, 0.0625, ((1, 128),))
    w_down = bell_draw(streams_of[11], (EXP_W * HID, D), HID ** -0.5, 0.1875, ((0, 128),))
    return dict(queries=queries, latent_cache=latent_cache, cache_lengths=cache_lengths, residual=residual, value_up=value_up, out_proj=out_proj, norm_gain=norm_gain, expert_ids=expert_ids, route_weights=route_weights, w_gate=w_gate, w_up=w_up, w_down=w_down)


score_scale = 192.0 ** (-0.5)
norm_eps = 1e-06

def slot_tables(route_ids, weights_given, experts_window, capacity):
    matches = route_ids[:, :, None] == jnp.arange(experts_window, dtype=jnp.int32)[None, None, :]
    chosen = jnp.any(matches, axis=1).astype(jnp.int32)
    position = jnp.cumsum(chosen, axis=0) - chosen
    slot_hit = (position[:, :, None] == jnp.arange(capacity, dtype=jnp.int32)[None, None, :]) & (chosen[:, :, None] > 0)
    weight_te = lax.optimization_barrier(jnp.sum(jnp.where(matches, weights_given[:, :, None], jnp.float32(0.0)), axis=1))
    return (slot_hit, weight_te)

def attend_one(operands):
    query, cache, length = operands
    scores = jnp.dot(query, cache.T, preferred_element_type=jnp.float32) * score_scale
    valid = jnp.arange(cache.shape[0], dtype=jnp.int32) < length
    scores = jnp.where(valid[None, :], scores, jnp.float32(-1e+30))
    attn_weights = jax.nn.softmax(scores, axis=-1).astype(jnp.bfloat16)
    return jnp.dot(attn_weights, cache[:, :LATENT], preferred_element_type=jnp.float32).astype(jnp.bfloat16)

def reference(queries, latent_cache, cache_lengths, residual, value_up, out_proj, norm_gain, expert_ids, route_weights, w_gate, w_up, w_down):
    contexts = lax.map(attend_one, (queries, latent_cache, cache_lengths))
    values = jnp.einsum('rhl,hlv->rhv', contexts.astype(jnp.float32), value_up.astype(jnp.float32)).astype(jnp.bfloat16)
    attended = jnp.dot(values.reshape(REQS, HEADS * VDIM), out_proj, preferred_element_type=jnp.float32)
    hidden = residual.astype(jnp.float32) + attended
    mean_square = lax.optimization_barrier(jnp.mean(hidden * hidden, axis=1, keepdims=True))
    normed = (hidden * lax.rsqrt(mean_square + norm_eps) * norm_gain.astype(jnp.float32)).astype(jnp.bfloat16)
    tables = []
    gathered = []
    for side_index in range(N_SIDE):
        lower = side_index * GROUP
        slot_hit, weight_te = slot_tables(expert_ids[lower:lower + GROUP], route_weights[lower:lower + GROUP], EXP_W, CAP)
        tables.append((slot_hit, weight_te))
        picked = jnp.einsum('tec,td->ecd', slot_hit.astype(jnp.float32), normed[lower:lower + GROUP].astype(jnp.float32))
        gathered.append(picked.astype(jnp.bfloat16))
    token_rows = jnp.concatenate(gathered, axis=1)

    def expert_apply(expert_index):
        rows_here = lax.dynamic_index_in_dim(token_rows, expert_index, 0, keepdims=False)
        gate_cols = lax.dynamic_slice_in_dim(w_gate, expert_index * HID, HID, 1)
        up_cols = lax.dynamic_slice_in_dim(w_up, expert_index * HID, HID, 1)
        down_rows = lax.dynamic_slice_in_dim(w_down, expert_index * HID, HID, 0)
        gate_part = jnp.dot(rows_here, gate_cols, preferred_element_type=jnp.float32)
        up_part = jnp.dot(rows_here, up_cols, preferred_element_type=jnp.float32)
        activated = (jax.nn.silu(gate_part) * up_part).astype(jnp.bfloat16)
        return jnp.dot(activated, down_rows, preferred_element_type=jnp.float32)
    expert_out = lax.map(expert_apply, jnp.arange(EXP_W, dtype=jnp.int32))
    results = []
    for side_index in range(N_SIDE):
        lower = side_index * GROUP
        slot_hit, weight_te = tables[side_index]
        combine = slot_hit.astype(jnp.float32) * weight_te[:, :, None]
        block_out = expert_out[:, side_index * CAP:(side_index + 1) * CAP]
        routed = jnp.einsum('tec,ecd->td', combine, block_out, precision=lax.Precision.HIGHEST)
        results.append((hidden[lower:lower + GROUP] + routed).astype(jnp.bfloat16))
    return jnp.concatenate(results, axis=0)
```

```python
import functools

import jax
import jax.numpy as jnp
from jax import lax
from jax.experimental import pallas as pl
from jax.experimental.pallas import tpu as pltpu
from jax.sharding import PartitionSpec as P

MESH = pl.DeviceIdType.MESH
LANES = 128
SCORE_SCALE = 192.0 ** (-0.5)
NORM_EPS = 1e-06
BF16 = jnp.bfloat16
F32 = jnp.float32


def nt_dot(a, b):
    return lax.dot_general(a, b, (((1,), (1,)), ((), ())), preferred_element_type=F32)


def nn_dot(a, b):
    return jnp.dot(a, b, preferred_element_type=F32)


def layer_kernel(
    dims,
    q_ref,
    cache_ref,
    len_ref,
    res_ref,
    vu_ref,
    wo_ref,
    gain_ref,
    ids_ref,
    rw_ref,
    wg_ref,
    wu_ref,
    wd_ref,
    out_ref,
    cache_v,
    wg_v,
    wu_v,
    wd_v,
    wo_v,
    vu_v,
    ctx_f,
    ctx_send,
    ctx_recv,
    val_v,
    part_send,
    part_recv,
    part_own,
    res_v,
    hid_v,
    hid_t,
    pos_v,
    wte_v,
    onehot,
    wslot,
    disp,
    rows,
    osend,
    ret,
    cache_sem,
    weight_sem,
    wo_sem,
    wo_send_sem,
    wo_recv_sem,
    vu_sem,
    vu_send_sem,
    vu1_sem,
    vu2_sem,
    sib_send_sem,
    sib_recv_sem,
    ctx_send_sem,
    ctx_recv_sem,
    ag_send_sem,
    ag1_sem,
    ag2_sem,
    rs_send_sem,
    rs_recv_sem,
    disp_send_sem,
    disp_recv_sem,
    ret_send_sem,
    ret_recv_sem,
):
    side_n, nx, nz = dims["side"], dims["x"], dims["z"]
    ny = nx
    plane = nx * ny
    ndev = plane * nz
    reqs, heads, _ = q_ref.shape
    length = cache_ref.shape[2]
    latent = vu_ref.shape[1]
    vdim = vu_ref.shape[2]
    cols = res_ref.shape[0]
    tokens = res_ref.shape[1]
    blk = nz * reqs
    chunk = ny * blk
    half = plane // side_n
    experts = side_n * plane
    cap = onehot.shape[0] // experts
    full = ndev * cols
    side = lax.axis_index("side")
    dev = lax.axis_index("dev")
    x = dev // (ny * nz)
    y = (dev // nz) % ny
    z = dev % nz
    own_block = x * ny + y
    up = jnp.where(side == 0, x, y)
    uq = jnp.where(side == 0, y, x)
    twin = 1 - side

    def block_of(w, u):
        return jnp.where(side == 0, w * ny + u, u * ny + w)

    def at_plane(block):
        return {"side": side, "dev": block * nz + z}

    def at_ring(zz):
        return {"side": side, "dev": own_block * nz + zz}

    def remote(src, dst, send, recv, target):
        return pltpu.make_async_remote_copy(
            src_ref=src, dst_ref=dst, send_sem=send, recv_sem=recv, device_id=target, device_id_type=MESH
        )

    def drain(ref, sem):
        pltpu.make_async_copy(ref, ref, sem).wait()

    def rows_at(start, size):
        return pl.ds(pl.multiple_of(start, size), size)

    for r in range(reqs):
        pltpu.make_async_copy(cache_ref.at[r], cache_v.at[r], cache_sem.at[r]).start()
    half_lanes = half * LANES
    half_rows = latent // side_n
    my_half = pl.ds(pl.multiple_of(side * half_lanes, half_lanes), half_lanes)
    my_rows = rows_at(side * half_rows, half_rows)

    def wo_source(j, zz):
        return wo_ref.at[:, rows_at((j * nz + zz) * LANES, LANES)]

    def wo_place(zz, j):
        return wo_v.at[zz, pl.ds(0, cols), rows_at(j * LANES, LANES)]

    for zz in range(nz):
        wo_v[zz, cols:, :] = jnp.zeros((LANES - cols, plane * LANES), BF16)
    for i in range(half):
        j = side * half + i
        pltpu.make_async_copy(wo_source(j, z), wo_place(z, j), wo_sem).start()
    own_vu = pltpu.make_async_copy(vu_ref.at[0, my_rows, :], vu_v.at[own_block, my_rows, :], vu_sem)
    own_vu.start()
    pltpu.make_async_copy(wg_ref, wg_v.at[:, pl.ds(0, cols), :], weight_sem.at[0]).start()
    pltpu.make_async_copy(wu_ref, wu_v.at[:, pl.ds(0, cols), :], weight_sem.at[1]).start()
    pltpu.make_async_copy(wd_ref, wd_v, weight_sem.at[2]).start()

    barrier = pltpu.get_barrier_semaphore()

    def greet(i, carry):
        other = lax.rem(side * ndev + dev + i, side_n * ndev)
        pl.semaphore_signal(
            barrier, inc=1, device_id={"side": other // ndev, "dev": other % ndev}, device_id_type=MESH
        )
        return carry

    lax.fori_loop(1, side_n * ndev, greet, 0)

    def attend(r):
        pltpu.make_async_copy(cache_ref.at[r], cache_v.at[r], cache_sem.at[r]).wait()
        scores = nn_dot(q_ref[r], cache_v[r]) * SCORE_SCALE
        valid = lax.broadcasted_iota(jnp.int32, scores.shape, 1) < len_ref[r]
        scores = jnp.where(valid, scores, -1e30)
        weights = jnp.exp(scores - jnp.max(scores, axis=1, keepdims=True))
        weights = (weights / jnp.sum(weights, axis=1, keepdims=True)).astype(BF16)
        context = nt_dot(weights, cache_v[r, 0:latent, :])
        for b in range(latent // LANES):
            ctx_f[b, r * heads : (r + 1) * heads, :] = context[:, b * LANES : (b + 1) * LANES]

    quarter = reqs // 4
    for r in range(quarter):
        attend(r)

    pl.semaphore_wait(barrier, side_n * ndev - 1)
    for k in range(1, nx):
        remote(
            vu_ref.at[0, my_rows, :],
            vu_v.at[own_block, my_rows, :],
            vu_send_sem,
            vu1_sem.at[k - 1],
            at_plane(block_of(up, (uq + k) % ny)),
        ).start()
    for k in range(1, nz):
        to = (z + k) % nz
        for i in range(half):
            j = side * half + i
            remote(wo_source(j, to), wo_place(z, j), wo_send_sem, wo_recv_sem.at[k - 1], at_ring(to)).start()
    own_vu.wait()

    def forward_vu(a):
        block = block_of(up, (uq + ny - a) % ny)
        piece = vu_v.at[block, my_rows, :]
        if a > 0:
            pltpu.make_async_copy(piece, piece, vu1_sem.at[a - 1]).wait()
        for k in range(1, nx):
            to = at_plane(block_of((up + k) % nx, uq))
            remote(piece, piece, vu_send_sem, vu2_sem.at[k - 1, a], to).start()

    forward_vu(0)
    for r in range(quarter, 2 * quarter):
        attend(r)
    for a in range(1, ny):
        forward_vu(a)
    for r in range(2 * quarter, reqs):
        attend(r)

    def pack(jp, zz):
        parts = []
        for j in (2 * jp, 2 * jp + 1):
            pieces = [
                ctx_f[b, pl.ds(j * nz + zz, reqs, stride=heads), :] for b in range(latent // LANES)
            ]
            parts.append(jnp.concatenate(pieces, axis=1))
        return jnp.concatenate(parts, axis=0).astype(BF16)

    for zz in range(nz):
        for jp in range(plane // 2):
            ctx_send[zz, jp * 2 * reqs : (jp + 1) * 2 * reqs, :] = pack(jp, zz)
    for k in range(1, nz):
        to = (z + k) % nz
        remote(ctx_send.at[to], ctx_recv.at[z], ctx_send_sem, ctx_recv_sem.at[k - 1], at_ring(to)).start()
    ctx_recv[z] = ctx_send[z]

    for k in range(1, nx):
        for a in range(ny):
            piece = vu_v.at[block_of((up + nx - k) % nx, (uq + ny - a) % ny), my_rows, :]
            pltpu.make_async_copy(piece, piece, vu2_sem.at[k - 1, a]).wait()
    mate = {"side": twin, "dev": dev}
    vu_half = vu_v.at[:, my_rows, :]
    vu_swap = remote(vu_half, vu_half, sib_send_sem.at[0], sib_recv_sem.at[0], mate)
    vu_swap.start()
    wo_half = wo_v.at[:, :, my_half]
    own_wo = wo_v.at[z, pl.ds(0, cols), my_half]
    pltpu.make_async_copy(own_wo, own_wo, wo_sem).wait()
    for k in range(1, nz):
        piece = wo_v.at[(z + nz - k) % nz, pl.ds(0, cols), my_half]
        pltpu.make_async_copy(piece, piece, wo_recv_sem.at[k - 1]).wait()
    wo_swap = remote(wo_half, wo_half, sib_send_sem.at[1], sib_recv_sem.at[1], mate)
    wo_swap.start()

    ids = ids_ref[...]
    rw = rw_ref[...]
    expert_no = lax.broadcasted_iota(jnp.int32, (experts, tokens), 0)
    chosen = jnp.zeros((experts, tokens), F32)
    wte = jnp.zeros((experts, tokens), F32)
    for k in range(ids.shape[0]):
        match = ids[k : k + 1, :] == expert_no
        chosen = jnp.where(match, 1.0, chosen)
        wte = wte + jnp.where(match, rw[k : k + 1, :], 0.0)
    before = lax.broadcasted_iota(jnp.int32, (tokens, tokens), 0) < lax.broadcasted_iota(
        jnp.int32, (tokens, tokens), 1
    )
    position = nn_dot(chosen.astype(BF16), jnp.where(before, 1.0, 0.0).astype(BF16))
    pos_v[...] = jnp.where(chosen > 0.0, position, -1.0)
    wte_v[...] = wte

    def fill(e, carry):
        slot = lax.broadcasted_iota(jnp.int32, (cap, tokens), 0).astype(F32)
        hit = pos_v[pl.ds(e, 1), :] == slot
        onehot[rows_at(e * cap, cap), :] = jnp.where(hit, 1.0, 0.0).astype(BF16)
        picked = jnp.sum(jnp.where(hit, wte_v[pl.ds(e, 1), :], 0.0), axis=1, keepdims=True)
        wslot[rows_at(e * cap, cap), :] = jnp.broadcast_to(picked, (cap, LANES))
        return carry

    lax.fori_loop(0, experts, fill, 0)
    res_t = jnp.concatenate(
        [res_ref[...].astype(F32), jnp.zeros((LANES - cols, tokens), F32)], axis=0
    )
    res_v[...] = res_t.T
    for d in range(ndev):
        wg_v[d, cols:, :] = jnp.zeros((LANES - cols, wg_v.shape[2]), BF16)
        wu_v[d, cols:, :] = jnp.zeros((LANES - cols, wu_v.shape[2]), BF16)
    part_recv[z] = jnp.zeros((tokens, LANES), BF16)

    vu_swap.wait_recv()
    for k in range(1, nz):
        piece = ctx_recv.at[(z + nz - k) % nz]
        pltpu.make_async_copy(piece, piece, ctx_recv_sem.at[k - 1]).wait()
    my_block = rows_at(own_block * blk, blk)
    two = 2 * reqs
    for jp in range(plane // 2):
        lhs = jnp.concatenate([ctx_recv[zz, jp * two : (jp + 1) * two, :] for zz in range(nz)], axis=0)
        rhs = jnp.concatenate([vu_v[2 * jp], vu_v[2 * jp + 1]], axis=1)
        both = nn_dot(lhs, rhs)
        picked = [
            jnp.concatenate(
                [
                    both[zz * two : zz * two + reqs, 0:vdim],
                    both[zz * two + reqs : (zz + 1) * two, vdim : 2 * vdim],
                ],
                axis=1,
            )
            for zz in range(nz)
        ]
        val_v[my_block, jp * 2 * vdim : (jp + 1) * 2 * vdim] = jnp.concatenate(picked, axis=0).astype(BF16)

    mine = val_v.at[my_block, :]
    for k in range(1, ny):
        remote(mine, mine, ag_send_sem, ag1_sem.at[k - 1], at_plane(block_of(up, (uq + k) % ny))).start()
    for a in range(ny):
        piece = val_v.at[rows_at(block_of(up, (uq + ny - a) % ny) * blk, blk), :]
        if a > 0:
            pltpu.make_async_copy(piece, piece, ag1_sem.at[a - 1]).wait()
        for k in range(1, nx):
            to = at_plane(block_of((up + k) % nx, uq))
            remote(piece, piece, ag_send_sem, ag2_sem.at[k - 1, a], to).start()
    wo_swap.wait_recv()
    for k in range(nx):
        w = (up + nx - k) % nx
        if k > 0:
            for a in range(ny):
                piece = val_v.at[rows_at(block_of(w, (uq + ny - a) % ny) * blk, blk), :]
                pltpu.make_async_copy(piece, piece, ag2_sem.at[k - 1, a]).wait()
        lhs = jnp.concatenate([val_v[rows_at(block_of(w, u) * blk, blk), :] for u in range(ny)], axis=0)
        at = rows_at(w * chunk, chunk)
        own = jnp.zeros((chunk, LANES), F32)
        for zz in range(nz):
            part = nt_dot(lhs, wo_v[zz])
            own = jnp.where(z == zz, part, own)
            part_send[zz, at, :] = part.astype(BF16)
        part_own[at, :] = own
        for kk in range(1, nz):
            to = (z + kk) % nz
            remote(
                part_send.at[to, at, :], part_recv.at[z, at, :], rs_send_sem, rs_recv_sem.at[kk - 1, k], at_ring(to)
            ).start()
    for k in range(nx):
        at = rows_at(((up + nx - k) % nx) * chunk, chunk)
        for kk in range(1, nz):
            piece = part_recv.at[(z + nz - kk) % nz, at, :]
            pltpu.make_async_copy(piece, piece, rs_recv_sem.at[kk - 1, k]).wait()
    for w in range(nx):
        for u in range(ny):
            here = (w * ny + u) * blk
            total = part_own[here : here + blk, :]
            for zz in range(nz):
                total = total + part_recv[zz, here : here + blk, :].astype(F32)
            there = rows_at(block_of(w, u) * blk, blk)
            hid_v[there, :] = total + res_v[there, :]

    hidden = hid_v[...]
    squares = jnp.sum(hidden * hidden, axis=1, keepdims=True)
    high = squares.astype(BF16).astype(F32)
    middle = (squares - high).astype(BF16).astype(F32)
    low = squares - high - middle
    lane = lax.broadcasted_iota(jnp.int32, (tokens, LANES), 1)
    gain = jnp.concatenate([gain_ref[...].astype(F32), jnp.zeros((1, LANES - cols), F32)], axis=1)
    extended = hidden * gain
    extended = jnp.where(lane == cols, high, extended)
    extended = jnp.where(lane == cols + 1, middle, extended)
    extended = jnp.where(lane == cols + 2, low, extended)
    disp[...] = nn_dot(onehot[...], extended.astype(BF16)).astype(BF16)

    my_lanes = rows_at(dev * LANES, LANES)
    my_slots = rows_at(side * cap, cap)

    def dispatch(i, carry):
        ds = i // ndev
        dd = i % ndev
        sx = (x + dd // (ny * nz)) % nx
        sy = (y + (dd // nz) % ny) % ny
        sz = (z + dd % nz) % nz
        ss = (side + ds) % side_n
        expert = ss * plane + sx * ny + sy
        src = disp.at[rows_at(expert * cap, cap), :]
        remote(
            src,
            rows.at[my_slots, my_lanes],
            disp_send_sem,
            disp_recv_sem.at[x],
            {"side": ss, "dev": (sx * ny + sy) * nz + sz},
        ).start()
        return carry

    own_expert = side * plane + own_block
    pltpu.make_async_copy(
        disp.at[rows_at(own_expert * cap, cap), :], rows.at[my_slots, my_lanes], disp_recv_sem.at[x]
    ).start()
    lax.fori_loop(1, side_n * ndev, dispatch, 0)
    hid_t[...] = hidden.T
    pltpu.make_async_copy(wg_ref, wg_v.at[:, pl.ds(0, cols), :], weight_sem.at[0]).wait()
    pltpu.make_async_copy(wu_ref, wu_v.at[:, pl.ds(0, cols), :], weight_sem.at[1]).wait()
    pltpu.make_async_copy(wd_ref, wd_v, weight_sem.at[2]).wait()

    units = wg_v.shape[2]
    group = ny * nz
    slots = side_n * cap
    gate = jnp.zeros((slots, units), F32)
    upward = jnp.zeros((slots, units), F32)
    marks = jnp.zeros((slots, LANES), F32)
    for k in range(nx):
        sx = (x + nx - k) % nx
        piece = rows.at[:, pl.ds(pl.multiple_of(sx * group * LANES, group * LANES), group * LANES)]
        pltpu.make_async_copy(piece, piece, disp_recv_sem.at[sx]).wait()
        lhs = piece[...]
        gate = gate + nn_dot(lhs, wg_v[pl.ds(sx * group, group)].reshape(group * LANES, units))
        upward = upward + nn_dot(lhs, wu_v[pl.ds(sx * group, group)].reshape(group * LANES, units))
        for d in range(group):
            marks = marks + lhs[:, d * LANES : (d + 1) * LANES].astype(F32)
    mark_lane = lax.broadcasted_iota(jnp.int32, (slots, LANES), 1)
    marks = jnp.where((mark_lane >= cols) & (mark_lane < cols + 3), marks, 0.0)
    scale = lax.rsqrt(jnp.sum(marks, axis=1, keepdims=True) / full + NORM_EPS)
    gate = gate * scale
    activated = (gate / (1.0 + jnp.exp(-gate)) * (upward * scale)).astype(BF16)

    per = 8
    groups = ndev // per
    first = dev // per
    home = rows_at(own_expert * cap, cap)

    def give(i, carry):
        g = (first + i) % groups
        width = per * cols
        out = nn_dot(activated, wd_v[:, pl.ds(pl.multiple_of(g * width, LANES), width)])
        for k in range(per):
            piece = out[:, k * cols : (k + 1) * cols]
            piece = jnp.concatenate([piece, jnp.zeros((slots, LANES - cols), F32)], axis=1)
            osend[:, rows_at((g * per + k) * LANES, LANES)] = piece.astype(BF16)
        for k in range(per):
            for s in range(side_n):
                target = g * per + k
                src = osend.at[s * cap : (s + 1) * cap, rows_at(target * LANES, LANES)]
                here = (side == s) & (dev == target)

                @pl.when(here)
                def _():
                    pltpu.make_async_copy(src, ret.at[z, home, :], ret_recv_sem).start()

                @pl.when(jnp.logical_not(here))
                def _():
                    remote(src, ret.at[z, home, :], ret_send_sem, ret_recv_sem, {"side": s, "dev": target}).start()

        return carry

    lax.fori_loop(0, groups, give, 0)

    drain(ret, ret_recv_sem)
    total = ret[0].astype(F32)
    for zz in range(1, nz):
        total = total + ret[zz].astype(F32)
    total = (total * wslot[...]).T
    high = total.astype(BF16)
    low = (total - high.astype(F32)).astype(BF16)
    routed = nn_dot(jnp.concatenate([high, low], axis=0), onehot[...])
    result = hid_t[...] + routed[0:LANES] + routed[LANES : 2 * LANES]
    out_ref[...] = result[0:cols].astype(BF16)

    drain(wo_v.at[0 : nz - 1, pl.ds(0, cols), my_half], wo_send_sem)
    drain(vu_v.at[0 : (nx - 1) * (ny + 1), my_rows, :], vu_send_sem)
    vu_swap.wait_send()
    wo_swap.wait_send()
    drain(ctx_send.at[0 : nz - 1], ctx_send_sem)
    drain(val_v.at[0 : (nx - 1) * (ny + 1) * blk], ag_send_sem)
    drain(part_send.at[0 : nz - 1], rs_send_sem)
    flat = side_n * ndev - 1
    drain(disp_drain_ref(ret, flat, cap), disp_send_sem)
    drain(disp_drain_ref(ret, flat, cap), ret_send_sem)


def disp_drain_ref(ret, blocks, cap):
    return ret.reshape(ret.shape[0] * ret.shape[1], ret.shape[2]).at[0 : blocks * cap]


def per_device(
    queries,
    latent_cache,
    cache_lengths,
    residual,
    value_up,
    out_proj,
    norm_gain,
    expert_ids,
    route_weights,
    w_gate,
    w_up,
    w_down,
):
    side_n = lax.axis_size("side")
    ndev = lax.axis_size("dev")
    nx = round(ndev ** (1 / 3))
    nz = nx
    plane = nx * nx
    tokens, cols = residual.shape
    reqs, heads, width = queries.shape
    length = latent_cache.shape[1]
    latent, vdim = value_up.shape[1:]
    units = w_gate.shape[1]
    experts = side_n * plane
    cap = 32
    blk = nz * reqs
    vmem = pl.BlockSpec(memory_space=pltpu.VMEM)
    smem = pl.BlockSpec(memory_space=pltpu.SMEM)
    hbm = pl.BlockSpec(memory_space=pl.ANY)
    dma = pltpu.SemaphoreType.DMA
    out = pl.pallas_call(
        functools.partial(layer_kernel, {"side": side_n, "x": nx, "z": nz}),
        out_shape=jax.ShapeDtypeStruct((cols, tokens), BF16),
        in_specs=[vmem, hbm, smem, vmem, hbm, hbm, vmem, vmem, vmem, hbm, hbm, hbm],
        out_specs=vmem,
        scratch_shapes=[
            pltpu.VMEM((reqs, width, length), BF16),
            pltpu.VMEM((ndev, LANES, units), BF16),
            pltpu.VMEM((ndev, LANES, units), BF16),
            pltpu.VMEM((units, ndev * cols), BF16),
            pltpu.VMEM((nz, LANES, plane * LANES), BF16),
            pltpu.VMEM((plane, latent, vdim), BF16),
            pltpu.VMEM((latent // LANES, reqs * heads, LANES), F32),
            pltpu.VMEM((nz, plane * reqs, latent), BF16),
            pltpu.VMEM((nz, plane * reqs, latent), BF16),
            pltpu.VMEM((tokens, plane * LANES), BF16),
            pltpu.VMEM((nz, tokens, LANES), BF16),
            pltpu.VMEM((nz, tokens, LANES), BF16),
            pltpu.VMEM((tokens, LANES), F32),
            pltpu.VMEM((tokens, LANES), F32),
            pltpu.VMEM((tokens, LANES), F32),
            pltpu.VMEM((LANES, tokens), F32),
            pltpu.VMEM((experts, tokens), F32),
            pltpu.VMEM((experts, tokens), F32),
            pltpu.VMEM((experts * cap, tokens), BF16),
            pltpu.VMEM((experts * cap, LANES), F32),
            pltpu.VMEM((experts * cap, LANES), BF16),
            pltpu.VMEM((side_n * cap, ndev * LANES), BF16),
            pltpu.VMEM((side_n * cap, ndev * LANES), BF16),
            pltpu.VMEM((nz, experts * cap, LANES), BF16),
            dma((reqs,)),
            dma((3,)),
            dma(()),
            dma(()),
            dma((nz - 1,)),
            dma(()),
            dma(()),
            dma((nx - 1,)),
            dma((nx - 1, nx)),
            dma((2,)),
            dma((2,)),
            dma(()),
            dma((nz - 1,)),
            dma(()),
            dma((nx - 1,)),
            dma((nx - 1, nx)),
            dma(()),
            dma((nz - 1, nx)),
            dma(()),
            dma((nx,)),
            dma(()),
            dma(()),
        ],
        compiler_params=pltpu.CompilerParams(
            collective_id=0, has_side_effects=True, vmem_limit_bytes=56 * 1024 * 1024
        ),
    )(
        queries,
        latent_cache.transpose(0, 2, 1),
        cache_lengths,
        residual.T,
        value_up,
        out_proj.T,
        norm_gain.reshape(1, cols),
        expert_ids.T,
        route_weights.T,
        w_gate.reshape(ndev, cols, units),
        w_up.reshape(ndev, cols, units),
        w_down,
    )
    return out.T


def solution(mesh):
    placed = (
        P(("side", "dev"), None, None),
        P(("side", "dev"), None, None),
        P(("side", "dev")),
        P("side", "dev"),
        P("dev", None, None),
        P(None, "dev"),
        P("dev"),
        P("side", None),
        P("side", None),
        P(None, ("side", "dev")),
        P(None, ("side", "dev")),
        P(("side", "dev"), None),
    )
    return jax.shard_map(
        per_device, mesh=mesh, in_specs=placed, out_specs=P("side", "dev"), check_vma=False
    )
```

```python
import functools

import jax
import jax.numpy as jnp
from jax import lax
from jax.experimental import pallas as pl
from jax.experimental.pallas import tpu as pltpu
from jax.sharding import PartitionSpec as P

MESH = pl.DeviceIdType.MESH
LANES = 128
SCORE_SCALE = 192.0 ** (-0.5)
NORM_EPS = 1e-06
BF16 = jnp.bfloat16
F32 = jnp.float32


def nt_dot(a, b):
    return lax.dot_general(a, b, (((1,), (1,)), ((), ())), preferred_element_type=F32)


def nn_dot(a, b):
    return jnp.dot(a, b, preferred_element_type=F32)


def layer_kernel(
    dims,
    q_ref,
    cache_ref,
    len_ref,
    res_ref,
    vu_ref,
    wo_ref,
    gain_ref,
    ids_ref,
    rw_ref,
    wg_ref,
    wu_ref,
    wd_ref,
    out_ref,
    cache_v,
    wg_v,
    wu_v,
    wd_v,
    wo_v,
    vu_v,
    ctx_f,
    ctx_send,
    ctx_recv,
    val_v,
    part_send,
    part_recv,
    part_own,
    res_v,
    hid_v,
    hid_t,
    pos_v,
    wte_v,
    onehot,
    wslot,
    disp,
    rows,
    osend,
    ret,
    cache_sem,
    weight_sem,
    wo_sem,
    wo_send_sem,
    wo_recv_sem,
    vu_sem,
    vu_send_sem,
    vu1_sem,
    vu2_sem,
    vu_swap_send_sem,
    vu_swap_recv_sem,
    wo_swap_send_sem,
    wo_swap_recv_sem,
    ctx_send_sem,
    ctx_recv_sem,
    ag_send_sem,
    ag1_sem,
    ag2_sem,
    rs_send_sem,
    rs_recv_sem,
    disp_send_sem,
    disp_recv_sem,
    ret_send_sem,
    ret_recv_sem,
):
    side_n, nx, nz = dims["side"], dims["x"], dims["z"]
    ny = nx
    plane = nx * ny
    ndev = plane * nz
    reqs, heads, _ = q_ref.shape
    length = cache_ref.shape[2]
    latent = vu_ref.shape[1]
    vdim = vu_ref.shape[2]
    cols = res_ref.shape[0]
    tokens = res_ref.shape[1]
    blk = nz * reqs
    chunk = ny * blk
    half = plane // side_n
    experts = side_n * plane
    cap = onehot.shape[0] // experts
    full = ndev * cols
    side = lax.axis_index("side")
    dev = lax.axis_index("dev")
    x = dev // (ny * nz)
    y = (dev // nz) % ny
    z = dev % nz
    own_block = x * ny + y
    up = jnp.where(side == 0, x, y)
    uq = jnp.where(side == 0, y, x)
    twin = 1 - side

    def block_of(w, u):
        return jnp.where(side == 0, w * ny + u, u * ny + w)

    def at_plane(block):
        return {"side": side, "dev": block * nz + z}

    def at_ring(zz):
        return {"side": side, "dev": own_block * nz + zz}

    def remote(src, dst, send, recv, target):
        return pltpu.make_async_remote_copy(
            src_ref=src, dst_ref=dst, send_sem=send, recv_sem=recv, device_id=target, device_id_type=MESH
        )

    def drain(ref, sem):
        pltpu.make_async_copy(ref, ref, sem).wait()

    def rows_at(start, size):
        return pl.ds(pl.multiple_of(start, size), size)

    for r in range(reqs):
        pltpu.make_async_copy(cache_ref.at[r], cache_v.at[r], cache_sem.at[r]).start()
    half_lanes = half * LANES
    half_rows = latent // side_n
    my_half = pl.ds(pl.multiple_of(side * half_lanes, half_lanes), half_lanes)
    my_rows = rows_at(side * half_rows, half_rows)

    def wo_source(j, zz):
        return wo_ref.at[:, rows_at((j * nz + zz) * LANES, LANES)]

    def wo_place(zz, j):
        return wo_v.at[zz, pl.ds(0, cols), rows_at(j * LANES, LANES)]

    for zz in range(nz):
        wo_v[zz, cols:, :] = jnp.zeros((LANES - cols, plane * LANES), BF16)
    for i in range(half):
        j = side * half + i
        pltpu.make_async_copy(wo_source(j, z), wo_place(z, j), wo_sem).start()
    own_vu = pltpu.make_async_copy(vu_ref.at[0, my_rows, :], vu_v.at[own_block, my_rows, :], vu_sem)
    own_vu.start()
    pltpu.make_async_copy(wg_ref, wg_v.at[:, pl.ds(0, cols), :], weight_sem.at[0]).start()
    pltpu.make_async_copy(wu_ref, wu_v.at[:, pl.ds(0, cols), :], weight_sem.at[1]).start()
    pltpu.make_async_copy(wd_ref, wd_v, weight_sem.at[2]).start()

    barrier = pltpu.get_barrier_semaphore()
    mate = {"side": twin, "dev": dev}
    friends = [mate]
    for k in range(1, nx):
        friends.append({"side": side, "dev": (((x + k) % nx) * ny + y) * nz + z})
        friends.append({"side": side, "dev": (x * ny + (y + k) % ny) * nz + z})
        friends.append({"side": side, "dev": own_block * nz + (z + k) % nz})
    for friend in friends:
        pl.semaphore_signal(barrier, inc=1, device_id=friend, device_id_type=MESH)

    def attend(r):
        pltpu.make_async_copy(cache_ref.at[r], cache_v.at[r], cache_sem.at[r]).wait()
        scores = nn_dot(q_ref[r], cache_v[r]) * SCORE_SCALE
        valid = lax.broadcasted_iota(jnp.int32, scores.shape, 1) < len_ref[r]
        scores = jnp.where(valid, scores, -1e30)
        weights = jnp.exp(scores - jnp.max(scores, axis=1, keepdims=True))
        weights = (weights / jnp.sum(weights, axis=1, keepdims=True)).astype(BF16)
        context = nt_dot(weights, cache_v[r, 0:latent, :])
        for b in range(latent // LANES):
            ctx_f[b, r * heads : (r + 1) * heads, :] = context[:, b * LANES : (b + 1) * LANES]

    quarter = reqs // 4
    for r in range(quarter):
        attend(r)

    pl.semaphore_wait(barrier, len(friends))
    for k in range(1, nx):
        remote(
            vu_ref.at[0, my_rows, :],
            vu_v.at[own_block, my_rows, :],
            vu_send_sem,
            vu1_sem.at[k - 1],
            at_plane(block_of(up, (uq + k) % ny)),
        ).start()
    part_n = 2
    step = half // part_n
    part_lanes = step * LANES

    def lanes_of(part):
        return pl.ds(pl.multiple_of(side * half_lanes + part * part_lanes, part_lanes), part_lanes)

    def exchange_wo(part):
        for k in range(1, nz):
            to = (z + k) % nz
            for i in range(part * step, (part + 1) * step):
                j = side * half + i
                remote(
                    wo_source(j, to), wo_place(z, j), wo_send_sem, wo_recv_sem.at[k - 1, part], at_ring(to)
                ).start()

    def swap_wo(part):
        for k in range(1, nz):
            drain(wo_v.at[(z + nz - k) % nz, pl.ds(0, cols), lanes_of(part)], wo_recv_sem.at[k - 1, part])
        piece = wo_v.at[:, :, lanes_of(part)]
        copy = remote(piece, piece, wo_swap_send_sem.at[part], wo_swap_recv_sem.at[part], mate)
        copy.start()
        return copy

    exchange_wo(0)
    own_vu.wait()

    def forward_vu(a):
        block = block_of(up, (uq + ny - a) % ny)
        piece = vu_v.at[block, my_rows, :]
        if a > 0:
            pltpu.make_async_copy(piece, piece, vu1_sem.at[a - 1]).wait()
        for k in range(1, nx):
            to = at_plane(block_of((up + k) % nx, uq))
            remote(piece, piece, vu_send_sem, vu2_sem.at[k - 1, a], to).start()

    forward_vu(0)
    for r in range(quarter, 2 * quarter):
        attend(r)
    for a in range(1, ny):
        forward_vu(a)
    for r in range(2 * quarter, reqs):
        attend(r)

    def pack(jp, zz):
        parts = []
        for j in (2 * jp, 2 * jp + 1):
            pieces = [
                ctx_f[b, pl.ds(j * nz + zz, reqs, stride=heads), :] for b in range(latent // LANES)
            ]
            parts.append(jnp.concatenate(pieces, axis=1))
        return jnp.concatenate(parts, axis=0).astype(BF16)

    for zz in range(nz):
        for jp in range(plane // 2):
            ctx_send[zz, jp * 2 * reqs : (jp + 1) * 2 * reqs, :] = pack(jp, zz)
    for k in range(1, nz):
        to = (z + k) % nz
        remote(ctx_send.at[to], ctx_recv.at[z], ctx_send_sem, ctx_recv_sem.at[k - 1], at_ring(to)).start()
    exchange_wo(1)
    ctx_recv[z] = ctx_send[z]

    for k in range(1, nx):
        for a in range(ny):
            piece = vu_v.at[block_of((up + nx - k) % nx, (uq + ny - a) % ny), my_rows, :]
            pltpu.make_async_copy(piece, piece, vu2_sem.at[k - 1, a]).wait()
    vu_half = vu_v.at[:, my_rows, :]
    vu_swap = remote(vu_half, vu_half, vu_swap_send_sem, vu_swap_recv_sem, mate)
    vu_swap.start()
    drain(wo_v.at[z, pl.ds(0, cols), my_half], wo_sem)
    wo_swaps = [swap_wo(0)]

    ids = ids_ref[...]
    rw = rw_ref[...]
    expert_no = lax.broadcasted_iota(jnp.int32, (experts, tokens), 0)
    chosen = jnp.zeros((experts, tokens), F32)
    wte = jnp.zeros((experts, tokens), F32)
    for k in range(ids.shape[0]):
        match = ids[k : k + 1, :] == expert_no
        chosen = jnp.where(match, 1.0, chosen)
        wte = wte + jnp.where(match, rw[k : k + 1, :], 0.0)
    before = lax.broadcasted_iota(jnp.int32, (tokens, tokens), 0) < lax.broadcasted_iota(
        jnp.int32, (tokens, tokens), 1
    )
    position = nn_dot(chosen.astype(BF16), jnp.where(before, 1.0, 0.0).astype(BF16))
    pos_v[...] = jnp.where(chosen > 0.0, position, -1.0)
    wte_v[...] = wte

    def fill(e, carry):
        slot = lax.broadcasted_iota(jnp.int32, (cap, tokens), 0).astype(F32)
        hit = pos_v[pl.ds(e, 1), :] == slot
        onehot[rows_at(e * cap, cap), :] = jnp.where(hit, 1.0, 0.0).astype(BF16)
        picked = jnp.sum(jnp.where(hit, wte_v[pl.ds(e, 1), :], 0.0), axis=1, keepdims=True)
        wslot[rows_at(e * cap, cap), :] = jnp.broadcast_to(picked, (cap, LANES))
        return carry

    lax.fori_loop(0, experts, fill, 0)
    res_t = jnp.concatenate(
        [res_ref[...].astype(F32), jnp.zeros((LANES - cols, tokens), F32)], axis=0
    )
    res_v[...] = res_t.T
    for d in range(ndev):
        wg_v[d, cols:, :] = jnp.zeros((LANES - cols, wg_v.shape[2]), BF16)
        wu_v[d, cols:, :] = jnp.zeros((LANES - cols, wu_v.shape[2]), BF16)
    part_recv[z] = jnp.zeros((tokens, LANES), BF16)

    vu_swap.wait_recv()
    for k in range(1, nz):
        piece = ctx_recv.at[(z + nz - k) % nz]
        pltpu.make_async_copy(piece, piece, ctx_recv_sem.at[k - 1]).wait()
    my_block = rows_at(own_block * blk, blk)
    two = 2 * reqs
    for jp in range(plane // 2):
        lhs = jnp.concatenate([ctx_recv[zz, jp * two : (jp + 1) * two, :] for zz in range(nz)], axis=0)
        rhs = jnp.concatenate([vu_v[2 * jp], vu_v[2 * jp + 1]], axis=1)
        both = nn_dot(lhs, rhs)
        picked = [
            jnp.concatenate(
                [
                    both[zz * two : zz * two + reqs, 0:vdim],
                    both[zz * two + reqs : (zz + 1) * two, vdim : 2 * vdim],
                ],
                axis=1,
            )
            for zz in range(nz)
        ]
        val_v[my_block, jp * 2 * vdim : (jp + 1) * 2 * vdim] = jnp.concatenate(picked, axis=0).astype(BF16)

    half_blk = blk // 2

    def block_rows(w, u, part=None):
        start = block_of(w, u) * blk
        if part is None:
            return val_v.at[rows_at(start, blk), :]
        return val_v.at[rows_at(start + part * half_blk, half_blk), :]

    ahead, behind = (up + 1) % nx, (up + nx - 1) % nx
    across = (up + 2) % nx
    u_ahead, u_behind, u_across = (uq + 1) % ny, (uq + ny - 1) % ny, (uq + 2) % ny

    def pass_u(piece, forward, sem):
        to = at_plane(block_of(up, u_ahead if forward else u_behind))
        remote(piece, piece, ag_send_sem, ag1_sem.at[sem], to).start()

    def pass_w(piece, forward, sem, a):
        to = at_plane(block_of(ahead if forward else behind, uq))
        remote(piece, piece, ag_send_sem, ag2_sem.at[sem, a], to).start()

    mine = block_rows(up, uq)
    pass_u(mine, True, 0)
    pass_u(mine, False, 1)
    pass_w(mine, True, 0, 0)
    pass_w(mine, False, 1, 0)
    us = [uq, u_behind, u_ahead, u_across]
    drain(block_rows(up, u_behind), ag1_sem.at[0])
    pass_u(block_rows(up, u_behind, 0), True, 2)
    drain(block_rows(up, u_ahead), ag1_sem.at[1])
    pass_u(block_rows(up, u_ahead, 1), False, 3)
    for a in (1, 2):
        pass_w(block_rows(up, us[a]), True, 0, a)
        pass_w(block_rows(up, us[a]), False, 1, a)
    drain(block_rows(up, u_across, 0), ag1_sem.at[2])
    drain(block_rows(up, u_across, 1), ag1_sem.at[3])
    pass_w(block_rows(up, u_across), True, 0, 3)
    pass_w(block_rows(up, u_across), False, 1, 3)

    def hand_on(a):
        drain(block_rows(behind, us[a]), ag2_sem.at[0, a])
        pass_w(block_rows(behind, us[a], 0), True, 2, a)
        drain(block_rows(ahead, us[a]), ag2_sem.at[1, a])
        pass_w(block_rows(ahead, us[a], 1), False, 3, a)

    hand_on(0)
    wo_swaps.append(swap_wo(1))
    for swap in wo_swaps:
        swap.wait_recv()
    for k in range(nx):
        w = (up, behind, ahead, across)[k]
        if k == 1:
            for a in range(1, ny):
                hand_on(a)
        if k == 3:
            for a in range(ny):
                drain(block_rows(across, us[a], 0), ag2_sem.at[2, a])
                drain(block_rows(across, us[a], 1), ag2_sem.at[3, a])
        lhs = jnp.concatenate([val_v[rows_at(block_of(w, u) * blk, blk), :] for u in range(ny)], axis=0)
        at = rows_at(w * chunk, chunk)
        own = jnp.zeros((chunk, LANES), F32)
        for zz in range(nz):
            part = nt_dot(lhs, wo_v[zz])
            own = jnp.where(z == zz, part, own)
            part_send[zz, at, :] = part.astype(BF16)
        part_own[at, :] = own
        for kk in range(1, nz):
            to = (z + kk) % nz
            remote(
                part_send.at[to, at, :], part_recv.at[z, at, :], rs_send_sem, rs_recv_sem.at[kk - 1, k], at_ring(to)
            ).start()
    for k in range(nx):
        at = rows_at((up, behind, ahead, across)[k] * chunk, chunk)
        for kk in range(1, nz):
            piece = part_recv.at[(z + nz - kk) % nz, at, :]
            pltpu.make_async_copy(piece, piece, rs_recv_sem.at[kk - 1, k]).wait()
    for w in range(nx):
        for u in range(ny):
            here = (w * ny + u) * blk
            total = part_own[here : here + blk, :]
            for zz in range(nz):
                total = total + part_recv[zz, here : here + blk, :].astype(F32)
            there = rows_at(block_of(w, u) * blk, blk)
            hid_v[there, :] = total + res_v[there, :]

    hidden = hid_v[...]
    squares = jnp.sum(hidden * hidden, axis=1, keepdims=True)
    high = squares.astype(BF16).astype(F32)
    middle = (squares - high).astype(BF16).astype(F32)
    low = squares - high - middle
    lane = lax.broadcasted_iota(jnp.int32, (tokens, LANES), 1)
    gain = jnp.concatenate([gain_ref[...].astype(F32), jnp.zeros((1, LANES - cols), F32)], axis=1)
    extended = hidden * gain
    extended = jnp.where(lane == cols, high, extended)
    extended = jnp.where(lane == cols + 1, middle, extended)
    extended = jnp.where(lane == cols + 2, low, extended)
    disp[...] = nn_dot(onehot[...], extended.astype(BF16)).astype(BF16)

    my_lanes = rows_at(dev * LANES, LANES)
    my_slots = rows_at(side * cap, cap)

    def partner(i):
        j = (i * 91) % (side_n * ndev)
        ss = (side + j // ndev) % side_n
        sx = (x + (j % ndev) // (ny * nz)) % nx
        sy = (y + (j // nz) % ny) % ny
        sz = (z + j % nz) % nz
        return ss, sx, sy, sz

    def dispatch(i, carry):
        ss, sx, sy, sz = partner(i)
        expert = ss * plane + sx * ny + sy
        src = disp.at[rows_at(expert * cap, cap), :]
        remote(
            src,
            rows.at[my_slots, my_lanes],
            disp_send_sem,
            disp_recv_sem.at[x],
            {"side": ss, "dev": (sx * ny + sy) * nz + sz},
        ).start()
        return carry

    own_expert = side * plane + own_block
    pltpu.make_async_copy(
        disp.at[rows_at(own_expert * cap, cap), :], rows.at[my_slots, my_lanes], disp_recv_sem.at[x]
    ).start()
    lax.fori_loop(1, side_n * ndev, dispatch, 0)
    hid_t[...] = hidden.T
    pltpu.make_async_copy(wg_ref, wg_v.at[:, pl.ds(0, cols), :], weight_sem.at[0]).wait()
    pltpu.make_async_copy(wu_ref, wu_v.at[:, pl.ds(0, cols), :], weight_sem.at[1]).wait()
    pltpu.make_async_copy(wd_ref, wd_v, weight_sem.at[2]).wait()

    units = wg_v.shape[2]
    group = ny * nz
    slots = side_n * cap
    gate = jnp.zeros((slots, units), F32)
    upward = jnp.zeros((slots, units), F32)
    marks = jnp.zeros((slots, LANES), F32)
    for k in range(nx):
        sx = (x + nx - k) % nx
        piece = rows.at[:, pl.ds(pl.multiple_of(sx * group * LANES, group * LANES), group * LANES)]
        pltpu.make_async_copy(piece, piece, disp_recv_sem.at[sx]).wait()
        lhs = piece[...]
        gate = gate + nn_dot(lhs, wg_v[pl.ds(sx * group, group)].reshape(group * LANES, units))
        upward = upward + nn_dot(lhs, wu_v[pl.ds(sx * group, group)].reshape(group * LANES, units))
        for d in range(group):
            marks = marks + lhs[:, d * LANES : (d + 1) * LANES].astype(F32)
    mark_lane = lax.broadcasted_iota(jnp.int32, (slots, LANES), 1)
    marks = jnp.where((mark_lane >= cols) & (mark_lane < cols + 3), marks, 0.0)
    scale = lax.rsqrt(jnp.sum(marks, axis=1, keepdims=True) / full + NORM_EPS)
    gate = gate * scale
    activated = (gate / (1.0 + jnp.exp(-gate)) * (upward * scale)).astype(BF16)

    per = 8
    groups = ndev // per
    home = rows_at(own_expert * cap, cap)

    def spread(g, carry):
        width = per * cols
        out = nn_dot(activated, wd_v[:, pl.ds(pl.multiple_of(g * width, LANES), width)])
        for k in range(per):
            piece = out[:, k * cols : (k + 1) * cols]
            piece = jnp.concatenate([piece, jnp.zeros((slots, LANES - cols), F32)], axis=1)
            osend[:, rows_at((g * per + k) * LANES, LANES)] = piece.astype(BF16)
        return carry

    lax.fori_loop(0, groups, spread, 0)
    pltpu.make_async_copy(osend.at[my_slots, my_lanes], ret.at[z, home, :], ret_recv_sem).start()

    def give(i, carry):
        ss, sx, sy, sz = partner(i)
        target = (sx * ny + sy) * nz + sz
        remote(
            osend.at[rows_at(ss * cap, cap), rows_at(target * LANES, LANES)],
            ret.at[z, home, :],
            ret_send_sem,
            ret_recv_sem,
            {"side": ss, "dev": target},
        ).start()
        return carry

    lax.fori_loop(1, side_n * ndev, give, 0)

    drain(ret, ret_recv_sem)
    total = ret[0].astype(F32)
    for zz in range(1, nz):
        total = total + ret[zz].astype(F32)
    total = (total * wslot[...]).T
    high = total.astype(BF16)
    low = (total - high.astype(F32)).astype(BF16)
    routed = nn_dot(jnp.concatenate([high, low], axis=0), onehot[...])
    result = hid_t[...] + routed[0:LANES] + routed[LANES : 2 * LANES]
    out_ref[...] = result[0:cols].astype(BF16)

    drain(wo_v.at[0 : nz - 1, pl.ds(0, cols), my_half], wo_send_sem)
    drain(vu_v.at[0 : (nx - 1) * (ny + 1), my_rows, :], vu_send_sem)
    vu_swap.wait_send()
    for swap in wo_swaps:
        swap.wait_send()
    drain(ctx_send.at[0 : nz - 1], ctx_send_sem)
    drain(val_v.at[0 : 3 * (ny + 1) * blk], ag_send_sem)
    drain(part_send.at[0 : nz - 1], rs_send_sem)
    flat = side_n * ndev - 1
    drain(disp_drain_ref(ret, flat, cap), disp_send_sem)
    drain(disp_drain_ref(ret, flat, cap), ret_send_sem)


def disp_drain_ref(ret, blocks, cap):
    return ret.reshape(ret.shape[0] * ret.shape[1], ret.shape[2]).at[0 : blocks * cap]


def per_device(
    queries,
    latent_cache,
    cache_lengths,
    residual,
    value_up,
    out_proj,
    norm_gain,
    expert_ids,
    route_weights,
    w_gate,
    w_up,
    w_down,
):
    side_n = lax.axis_size("side")
    ndev = lax.axis_size("dev")
    nx = 4
    nz = nx
    plane = nx * nx
    tokens, cols = residual.shape
    reqs, heads, width = queries.shape
    length = latent_cache.shape[1]
    latent, vdim = value_up.shape[1:]
    units = w_gate.shape[1]
    experts = side_n * plane
    cap = 32
    blk = nz * reqs
    vmem = pl.BlockSpec(memory_space=pltpu.VMEM)
    smem = pl.BlockSpec(memory_space=pltpu.SMEM)
    hbm = pl.BlockSpec(memory_space=pl.ANY)
    dma = pltpu.SemaphoreType.DMA
    out = pl.pallas_call(
        functools.partial(layer_kernel, {"side": side_n, "x": nx, "z": nz}),
        out_shape=jax.ShapeDtypeStruct((cols, tokens), BF16),
        in_specs=[vmem, hbm, smem, vmem, hbm, hbm, vmem, vmem, vmem, hbm, hbm, hbm],
        out_specs=vmem,
        scratch_shapes=[
            pltpu.VMEM((reqs, width, length), BF16),
            pltpu.VMEM((ndev, LANES, units), BF16),
            pltpu.VMEM((ndev, LANES, units), BF16),
            pltpu.VMEM((units, ndev * cols), BF16),
            pltpu.VMEM((nz, LANES, plane * LANES), BF16),
            pltpu.VMEM((plane, latent, vdim), BF16),
            pltpu.VMEM((latent // LANES, reqs * heads, LANES), F32),
            pltpu.VMEM((nz, plane * reqs, latent), BF16),
            pltpu.VMEM((nz, plane * reqs, latent), BF16),
            pltpu.VMEM((tokens, plane * LANES), BF16),
            pltpu.VMEM((nz, tokens, LANES), BF16),
            pltpu.VMEM((nz, tokens, LANES), BF16),
            pltpu.VMEM((tokens, LANES), F32),
            pltpu.VMEM((tokens, LANES), F32),
            pltpu.VMEM((tokens, LANES), F32),
            pltpu.VMEM((LANES, tokens), F32),
            pltpu.VMEM((experts, tokens), F32),
            pltpu.VMEM((experts, tokens), F32),
            pltpu.VMEM((experts * cap, tokens), BF16),
            pltpu.VMEM((experts * cap, LANES), F32),
            pltpu.VMEM((experts * cap, LANES), BF16),
            pltpu.VMEM((side_n * cap, ndev * LANES), BF16),
            pltpu.VMEM((side_n * cap, ndev * LANES), BF16),
            pltpu.VMEM((nz, experts * cap, LANES), BF16),
            dma((reqs,)),
            dma((3,)),
            dma(()),
            dma(()),
            dma((nz - 1, 2)),
            dma(()),
            dma(()),
            dma((nx - 1,)),
            dma((nx - 1, nx)),
            dma(()),
            dma(()),
            dma((2,)),
            dma((2,)),
            dma(()),
            dma((nz - 1,)),
            dma(()),
            dma((4,)),
            dma((4, nx)),
            dma(()),
            dma((nz - 1, nx)),
            dma(()),
            dma((nx,)),
            dma(()),
            dma(()),
        ],
        compiler_params=pltpu.CompilerParams(
            collective_id=0, has_side_effects=True, vmem_limit_bytes=56 * 1024 * 1024
        ),
    )(
        queries,
        latent_cache.transpose(0, 2, 1),
        cache_lengths,
        residual.T,
        value_up,
        out_proj.T,
        norm_gain.reshape(1, cols),
        expert_ids.T,
        route_weights.T,
        w_gate.reshape(ndev, cols, units),
        w_up.reshape(ndev, cols, units),
        w_down,
    )
    return out.T


def solution(mesh):
    placed = (
        P(("side", "dev"), None, None),
        P(("side", "dev"), None, None),
        P(("side", "dev")),
        P("side", "dev"),
        P("dev", None, None),
        P(None, "dev"),
        P("dev"),
        P("side", None),
        P("side", None),
        P(None, ("side", "dev")),
        P(None, ("side", "dev")),
        P(("side", "dev"), None),
    )
    return jax.shard_map(
        per_device, mesh=mesh, in_specs=placed, out_specs=P("side", "dev"), check_vma=False
    )
```

```python
import functools

import jax
import jax.numpy as jnp
from jax import lax
from jax.experimental import pallas as pl
from jax.experimental.pallas import tpu as pltpu
from jax.sharding import PartitionSpec as P

MESH = pl.DeviceIdType.MESH
LANES = 128
SCORE_SCALE = 192.0 ** (-0.5)
NORM_EPS = 1e-06
BF16 = jnp.bfloat16
F32 = jnp.float32


def nt_dot(a, b):
    return lax.dot_general(a, b, (((1,), (1,)), ((), ())), preferred_element_type=F32)


def nn_dot(a, b):
    return jnp.dot(a, b, preferred_element_type=F32)


def layer_kernel(
    dims,
    q_hbm,
    cache_ref,
    len_hbm,
    res_hbm,
    vu_ref,
    wo_ref,
    gain_hbm,
    ids_hbm,
    rw_hbm,
    wg_ref,
    wu_ref,
    wd_ref,
    out_ref,
    q_ref,
    len_ref,
    res_ref,
    gain_ref,
    ids_ref,
    rw_ref,
    cache_v,
    wg_v,
    wu_v,
    wd_v,
    wo_v,
    vu_v,
    ctx_f,
    ctx_send,
    ctx_recv,
    val_v,
    part_send,
    part_recv,
    part_own,
    res_v,
    hid_v,
    hid_t,
    pos_v,
    wte_v,
    onehot,
    wslot,
    disp,
    rows,
    osend,
    far_recv,
    near_send,
    near_recv,
    fin,
    ret,
    cache_sem,
    q_sem,
    small_sem,
    weight_sem,
    wo_sem,
    wo_send_sem,
    wo_recv_sem,
    vu_sem,
    vu_send_sem,
    vu1_sem,
    vu2_sem,
    vu_swap_send_sem,
    vu_swap_recv_sem,
    wo_swap_send_sem,
    wo_swap_recv_sem,
    ctx_send_sem,
    ctx_recv_sem,
    ag_send_sem,
    ag1_sem,
    ag2_sem,
    rs_send_sem,
    rs_recv_sem,
    disp_send_sem,
    disp_recv_sem,
    ring_send_sem,
    ring_recv_sem,
    far_send_sem,
    far_recv_sem,
    near_send_sem,
    near_recv_sem,
    ret_send_sem,
    ret_recv_sem,
):
    side_n, nx, nz = dims["side"], dims["x"], dims["z"]
    ny = nx
    plane = nx * ny
    ndev = plane * nz
    reqs, heads, _ = q_ref.shape
    length = cache_ref.shape[2]
    latent = vu_ref.shape[1]
    vdim = vu_ref.shape[2]
    cols = res_ref.shape[0]
    tokens = res_ref.shape[1]
    blk = nz * reqs
    chunk = ny * blk
    half = plane // side_n
    experts = side_n * plane
    cap = onehot.shape[0] // experts
    full = ndev * cols
    side = lax.axis_index("side")
    dev = lax.axis_index("dev")
    x = dev // (ny * nz)
    y = (dev // nz) % ny
    z = dev % nz
    own_block = x * ny + y
    up = jnp.where(side == 0, x, y)
    uq = jnp.where(side == 0, y, x)
    twin = 1 - side

    def block_of(w, u):
        return jnp.where(side == 0, w * ny + u, u * ny + w)

    def at_plane(block):
        return {"side": side, "dev": block * nz + z}

    def at_ring(zz):
        return {"side": side, "dev": own_block * nz + zz}

    def remote(src, dst, send, recv, target):
        return pltpu.make_async_remote_copy(
            src_ref=src, dst_ref=dst, send_sem=send, recv_sem=recv, device_id=target, device_id_type=MESH
        )

    def drain(ref, sem):
        pltpu.make_async_copy(ref, ref, sem).wait()

    def rows_at(start, size):
        return pl.ds(pl.multiple_of(start, size), size)

    for zz in range(nz):
        wo_v[zz, cols:, :] = jnp.zeros((LANES - cols, plane * LANES), BF16)
    barrier = pltpu.get_barrier_semaphore()
    mate = {"side": twin, "dev": dev}
    friends = [mate]
    for k in range(1, nx):
        friends.append({"side": side, "dev": (((x + k) % nx) * ny + y) * nz + z})
        friends.append({"side": side, "dev": (x * ny + (y + k) % ny) * nz + z})
        friends.append({"side": side, "dev": own_block * nz + (z + k) % nz})
    for friend in friends:
        pl.semaphore_signal(barrier, inc=1, device_id=friend, device_id_type=MESH)

    half_lanes = half * LANES
    half_rows = latent // side_n
    my_half = pl.ds(pl.multiple_of(side * half_lanes, half_lanes), half_lanes)
    my_rows = rows_at(side * half_rows, half_rows)

    def wo_source(j, zz):
        return wo_ref.at[:, rows_at((j * nz + zz) * LANES, LANES)]

    def wo_place(zz, j):
        return wo_v.at[zz, pl.ds(0, cols), rows_at(j * LANES, LANES)]

    for i in range(half):
        j = side * half + i
        pltpu.make_async_copy(wo_source(j, z), wo_place(z, j), wo_sem).start()
    own_vu = pltpu.make_async_copy(vu_ref.at[0, my_rows, :], vu_v.at[own_block, my_rows, :], vu_sem)
    own_vu.start()
    len_copy = pltpu.make_async_copy(len_hbm, len_ref, small_sem.at[0])
    len_copy.start()
    for r in range(reqs):
        pltpu.make_async_copy(q_hbm.at[r], q_ref.at[r], q_sem.at[r]).start()
        pltpu.make_async_copy(cache_ref.at[r], cache_v.at[r], cache_sem.at[r]).start()
    small_copies = [
        pltpu.make_async_copy(source, place, small_sem.at[n + 1])
        for n, (source, place) in enumerate(
            ((res_hbm, res_ref), (gain_hbm, gain_ref), (ids_hbm, ids_ref), (rw_hbm, rw_ref))
        )
    ]
    for copy in small_copies:
        copy.start()
    weight_copies = [pltpu.make_async_copy(wd_ref, wd_v, weight_sem.at[2, 0])]
    for zz in range(nz):
        for n, (source, place) in enumerate(((wg_ref, wg_v), (wu_ref, wu_v))):
            weight_copies.append(
                pltpu.make_async_copy(source.at[:, zz], place.at[zz, :, pl.ds(0, cols), :], weight_sem.at[n, zz])
            )

    def attend(r):
        pltpu.make_async_copy(q_hbm.at[r], q_ref.at[r], q_sem.at[r]).wait()
        pltpu.make_async_copy(cache_ref.at[r], cache_v.at[r], cache_sem.at[r]).wait()
        scores = nn_dot(q_ref[r], cache_v[r]) * SCORE_SCALE
        valid = lax.broadcasted_iota(jnp.int32, scores.shape, 1) < len_ref[r]
        scores = jnp.where(valid, scores, -1e30)
        weights = jnp.exp(scores - jnp.max(scores, axis=1, keepdims=True))
        weights = (weights / jnp.sum(weights, axis=1, keepdims=True)).astype(BF16)
        context = nt_dot(weights, cache_v[r, 0:latent, :])
        for b in range(latent // LANES):
            ctx_f[b, r * heads : (r + 1) * heads, :] = context[:, b * LANES : (b + 1) * LANES]

    pl.semaphore_wait(barrier, len(friends))
    for k in range(1, nx):
        remote(
            vu_ref.at[0, my_rows, :],
            vu_v.at[own_block, my_rows, :],
            vu_send_sem,
            vu1_sem.at[k - 1],
            at_plane(block_of(up, (uq + k) % ny)),
        ).start()
    cuts = (0, 3 * half // 8, half)

    def lanes_of(part):
        start = side * half_lanes + cuts[part] * LANES
        return pl.ds(pl.multiple_of(start, LANES), (cuts[part + 1] - cuts[part]) * LANES)

    def exchange_wo(part):
        for i in range(cuts[part], cuts[part + 1]):
            for k in range(1, nz):
                to = (z + k) % nz
                j = side * half + i
                remote(
                    wo_source(j, to), wo_place(z, j), wo_send_sem, wo_recv_sem.at[k - 1, part], at_ring(to)
                ).start()

    def swap_wo(part):
        for k in range(1, nz):
            drain(wo_v.at[(z + nz - k) % nz, pl.ds(0, cols), lanes_of(part)], wo_recv_sem.at[k - 1, part])
        piece = wo_v.at[:, :, lanes_of(part)]
        copy = remote(piece, piece, wo_swap_send_sem.at[part], wo_swap_recv_sem.at[part], mate)
        copy.start()
        return copy

    exchange_wo(0)

    def forward_vu(a):
        block = block_of(up, (uq + ny - a) % ny)
        piece = vu_v.at[block, my_rows, :]
        if a > 0:
            drain(piece, vu1_sem.at[a - 1])
        for k in range(1, nx):
            to = at_plane(block_of((up + k) % nx, uq))
            source = piece if a > 0 else vu_ref.at[0, my_rows, :]
            remote(source, piece, vu_send_sem, vu2_sem.at[k - 1, a], to).start()

    forward_vu(0)
    len_copy.wait()

    pairs = reqs // 2

    def send_contexts(g):
        for r in (2 * g, 2 * g + 1):
            for zz in range(nz):
                pieces = [
                    ctx_f[b, pl.ds(r * heads + zz, plane, stride=nz), :] for b in range(latent // LANES)
                ]
                ctx_send[zz, r * plane : (r + 1) * plane, :] = jnp.concatenate(pieces, axis=1).astype(BF16)
        at = pl.ds(2 * g * plane, 2 * plane)
        for k in range(1, nz):
            to = (z + k) % nz
            remote(
                ctx_send.at[to, at, :], ctx_recv.at[z, at, :], ctx_send_sem, ctx_recv_sem.at[k - 1, g], at_ring(to)
            ).start()

    for g in range(pairs):
        attend(2 * g)
        attend(2 * g + 1)
        send_contexts(g)
        if g == 1:
            for a in range(1, ny):
                forward_vu(a)
            for copy in weight_copies:
                copy.start()
    exchange_wo(1)
    ctx_recv[z] = ctx_send[z]

    def swap_vu(k):
        w = (up + nx - k) % nx
        for a in range(ny):
            block = block_of(w, (uq + ny - a) % ny)
            piece = vu_v.at[block, my_rows, :]
            if k == 0 and a == 0:
                own_vu.wait()
            elif k > 0:
                drain(piece, vu2_sem.at[k - 1, a])
            remote(piece, piece, vu_swap_send_sem, vu_swap_recv_sem, mate).start()

    for k in (0, 1, 3, 2):
        swap_vu(k)
    drain(wo_v.at[z, pl.ds(0, cols), my_half], wo_sem)
    wo_swaps = [swap_wo(0)]

    for copy in small_copies:
        copy.wait()
    ids = ids_ref[...]
    rw = rw_ref[...]
    expert_no = lax.broadcasted_iota(jnp.int32, (experts, tokens), 0)
    chosen = jnp.zeros((experts, tokens), F32)
    wte = jnp.zeros((experts, tokens), F32)
    for k in range(ids.shape[0]):
        match = ids[k : k + 1, :] == expert_no
        chosen = jnp.where(match, 1.0, chosen)
        wte = wte + jnp.where(match, rw[k : k + 1, :], 0.0)
    before = lax.broadcasted_iota(jnp.int32, (tokens, tokens), 0) < lax.broadcasted_iota(
        jnp.int32, (tokens, tokens), 1
    )
    position = nn_dot(chosen.astype(BF16), jnp.where(before, 1.0, 0.0).astype(BF16))
    pos_v[...] = jnp.where(chosen > 0.0, position, -1.0)
    wte_v[...] = wte

    def fill(e, carry):
        slot = lax.broadcasted_iota(jnp.int32, (cap, tokens), 0).astype(F32)
        hit = pos_v[pl.ds(e, 1), :] == slot
        onehot[rows_at(e * cap, cap), :] = jnp.where(hit, 1.0, 0.0).astype(BF16)
        picked = jnp.sum(jnp.where(hit, wte_v[pl.ds(e, 1), :], 0.0), axis=1, keepdims=True)
        wslot[rows_at(e * cap, cap), :] = jnp.broadcast_to(picked, (cap, LANES))
        return carry

    res_t = jnp.concatenate(
        [res_ref[...].astype(F32), jnp.zeros((LANES - cols, tokens), F32)], axis=0
    )
    res_v[...] = res_t.T
    for zz in range(nz):
        for j in range(plane):
            wg_v[zz, j, cols:, :] = jnp.zeros((LANES - cols, wg_v.shape[3]), BF16)
            wu_v[zz, j, cols:, :] = jnp.zeros((LANES - cols, wu_v.shape[3]), BF16)
    part_recv[z] = jnp.zeros((tokens, LANES), BF16)

    drain(vu_v.at[:, rows_at(twin * half_rows, half_rows), :], vu_swap_recv_sem)
    for k in range(1, nz):
        for g in range(pairs):
            drain(ctx_recv.at[(z + nz - k) % nz, pl.ds(2 * g * plane, 2 * plane), :], ctx_recv_sem.at[k - 1, g])
    my_block = rows_at(own_block * blk, blk)
    for zz in range(nz):
        for b in range(latent // LANES):
            ctx_f[b, zz * reqs * plane : (zz + 1) * reqs * plane, :] = ctx_recv[
                zz, :, b * LANES : (b + 1) * LANES
            ].astype(F32)
    for jp in range(plane // 2):
        lhs = [
            jnp.concatenate(
                [ctx_f[b, pl.ds(j, blk, stride=plane), :] for b in range(latent // LANES)], axis=1
            )
            for j in (2 * jp, 2 * jp + 1)
        ]
        rhs = jnp.concatenate([vu_v[2 * jp], vu_v[2 * jp + 1]], axis=1)
        both = nn_dot(jnp.concatenate(lhs, axis=0).astype(BF16), rhs)
        picked = jnp.concatenate([both[0:blk, 0:vdim], both[blk : 2 * blk, vdim : 2 * vdim]], axis=1)
        val_v[my_block, jp * 2 * vdim : (jp + 1) * 2 * vdim] = picked.astype(BF16)

    half_blk = blk // 2

    def block_rows(w, u, part=None):
        start = block_of(w, u) * blk
        if part is None:
            return val_v.at[rows_at(start, blk), :]
        return val_v.at[rows_at(start + part * half_blk, half_blk), :]

    ahead, behind = (up + 1) % nx, (up + nx - 1) % nx
    across = (up + 2) % nx
    u_ahead, u_behind, u_across = (uq + 1) % ny, (uq + ny - 1) % ny, (uq + 2) % ny

    def pass_u(piece, u, sem):
        remote(piece, piece, ag_send_sem, ag1_sem.at[sem], at_plane(block_of(up, u))).start()

    def pass_w(piece, forward, sem, a):
        to = at_plane(block_of(ahead if forward else behind, uq))
        remote(piece, piece, ag_send_sem, ag2_sem.at[sem, a], to).start()

    us = [uq, u_behind, u_ahead, u_across]
    mine = block_rows(up, uq)
    pass_u(mine, u_ahead, 0)
    pass_u(mine, u_behind, 1)
    pass_u(mine, u_across, 2)
    lax.fori_loop(0, experts // 4, fill, 0)
    pass_w(mine, True, 0, 0)
    pass_w(mine, False, 1, 0)
    lax.fori_loop(experts // 4, experts // 2, fill, 0)
    for a in range(1, ny):
        piece = block_rows(up, us[a])
        drain(piece, ag1_sem.at[a - 1])
        pass_w(piece, True, 0, a)
        pass_w(piece, False, 1, a)
        if a == 2:
            wo_swaps.append(swap_wo(1))

    def hand_on(a):
        drain(block_rows(behind, us[a]), ag2_sem.at[0, a])
        pass_w(block_rows(behind, us[a], 0), True, 2, a)
        drain(block_rows(ahead, us[a]), ag2_sem.at[1, a])
        pass_w(block_rows(ahead, us[a], 1), False, 3, a)

    def project(k):
        w = (up, behind, ahead, across)[k]
        lhs = jnp.concatenate([val_v[rows_at(block_of(w, u) * blk, blk), :] for u in range(ny)], axis=0)
        at = rows_at(w * chunk, chunk)
        own = jnp.zeros((chunk, LANES), F32)
        for zz in range(nz):
            part = nt_dot(lhs, wo_v[zz])
            own = jnp.where(z == zz, part, own)
            part_send[zz, at, :] = part.astype(BF16)
        part_own[at, :] = own
        for kk in range(1, nz):
            to = (z + kk) % nz
            remote(
                part_send.at[to, at, :], part_recv.at[z, at, :], rs_send_sem, rs_recv_sem.at[kk - 1, k], at_ring(to)
            ).start()

    hand_on(0)
    for swap in wo_swaps:
        swap.wait_recv()
    project(0)
    hand_on(1)
    hand_on(2)
    hand_on(3)
    project(1)
    project(2)
    lax.fori_loop(experts // 2, experts, fill, 0)
    for a in range(ny):
        drain(block_rows(across, us[a], 0), ag2_sem.at[2, a])
        drain(block_rows(across, us[a], 1), ag2_sem.at[3, a])
    project(3)
    for k in range(nx):
        at = rows_at((up, behind, ahead, across)[k] * chunk, chunk)
        for kk in range(1, nz):
            piece = part_recv.at[(z + nz - kk) % nz, at, :]
            pltpu.make_async_copy(piece, piece, rs_recv_sem.at[kk - 1, k]).wait()
    for w in range(nx):
        for u in range(ny):
            here = (w * ny + u) * blk
            total = part_own[here : here + blk, :]
            for zz in range(nz):
                total = total + part_recv[zz, here : here + blk, :].astype(F32)
            there = rows_at(block_of(w, u) * blk, blk)
            hid_v[there, :] = total + res_v[there, :]

    hidden = hid_v[...]
    squares = jnp.sum(hidden * hidden, axis=1, keepdims=True)
    high = squares.astype(BF16).astype(F32)
    middle = (squares - high).astype(BF16).astype(F32)
    low = squares - high - middle
    lane = lax.broadcasted_iota(jnp.int32, (tokens, LANES), 1)
    gain = jnp.concatenate([gain_ref[...].astype(F32), jnp.zeros((1, LANES - cols), F32)], axis=1)
    extended = hidden * gain
    extended = jnp.where(lane == cols, high, extended)
    extended = jnp.where(lane == cols + 1, middle, extended)
    extended = jnp.where(lane == cols + 2, low, extended)
    disp[...] = nn_dot(onehot[...], extended.astype(BF16)).astype(BF16)

    my_slots = rows_at(side * cap, cap)
    my_lanes = rows_at(own_block * LANES, LANES)
    own_expert = side * plane + own_block
    home = rows_at(own_expert * cap, cap)

    def dispatch(i, carry):
        ss = (side + i) % side_n
        sy = (y + (i // side_n) % ny) % ny
        dx = i // (side_n * ny)
        target = ((x + dx) % nx) * ny + sy
        remote(
            disp.at[rows_at((ss * plane + target) * cap, cap), :],
            rows.at[z, my_slots, my_lanes],
            disp_send_sem,
            disp_recv_sem.at[dx],
            {"side": ss, "dev": target * nz + z},
        ).start()
        return carry

    pltpu.make_async_copy(disp.at[home, :], rows.at[z, my_slots, my_lanes], disp_recv_sem.at[0]).start()
    lax.fori_loop(1, experts, dispatch, 0)
    hid_t[...] = hidden.T

    z_next, z_prev, z_far = (z + 1) % nz, (z + nz - 1) % nz, (z + 2) % nz
    width = ny * LANES
    slots = side_n * cap
    units = wg_v.shape[3]

    def lanes_from(p):
        return pl.ds(pl.multiple_of(p * width, width), width)

    def piece_of(zz, dx, part=None):
        lanes = lanes_from((x + nx - dx) % nx)
        if part is None:
            return rows.at[zz, :, lanes]
        return rows.at[zz, part * cap : (part + 1) * cap, lanes]

    for dx in range(nx):
        piece = piece_of(z, dx)
        drain(piece, disp_recv_sem.at[dx])
        remote(piece, piece, ring_send_sem, ring_recv_sem.at[0, dx], at_ring(z_next)).start()
        remote(piece, piece, ring_send_sem, ring_recv_sem.at[1, dx], at_ring(z_prev)).start()
    for copy in weight_copies:
        copy.wait()
    gate = jnp.zeros((slots, units), F32)
    upward = jnp.zeros((slots, units), F32)
    marks = jnp.zeros((slots, LANES), F32)

    def take(zz, gate, upward, marks):
        lhs = rows[zz]
        gate = gate + nn_dot(lhs, wg_v[zz].reshape(plane * LANES, units))
        upward = upward + nn_dot(lhs, wu_v[zz].reshape(plane * LANES, units))
        for j in range(plane):
            marks = marks + lhs[:, j * LANES : (j + 1) * LANES].astype(F32)
        return gate, upward, marks

    gate, upward, marks = take(z, gate, upward, marks)
    for dx in range(nx):
        drain(piece_of(z_prev, dx), ring_recv_sem.at[0, dx])
        piece = piece_of(z_prev, dx, 0)
        remote(piece, piece, ring_send_sem, ring_recv_sem.at[2, dx], at_ring(z_next)).start()
        drain(piece_of(z_next, dx), ring_recv_sem.at[1, dx])
        piece = piece_of(z_next, dx, 1)
        remote(piece, piece, ring_send_sem, ring_recv_sem.at[3, dx], at_ring(z_prev)).start()
    gate, upward, marks = take(z_prev, gate, upward, marks)
    gate, upward, marks = take(z_next, gate, upward, marks)
    for dx in range(nx):
        drain(piece_of(z_far, dx, 0), ring_recv_sem.at[2, dx])
        drain(piece_of(z_far, dx, 1), ring_recv_sem.at[3, dx])
    gate, upward, marks = take(z_far, gate, upward, marks)
    mark_lane = lax.broadcasted_iota(jnp.int32, (slots, LANES), 1)
    marks = jnp.where((mark_lane >= cols) & (mark_lane < cols + 3), marks, 0.0)
    scale = lax.rsqrt(jnp.sum(marks, axis=1, keepdims=True) / full + NORM_EPS)
    gate = gate * scale
    activated = (gate / (1.0 + jnp.exp(-gate)) * (upward * scale)).astype(BF16)

    top, low_half = pl.ds(0, cap), pl.ds(cap, cap)
    group = ny * nz * cols
    for k in range(nx):
        p = (x + k) % nx
        out = nn_dot(activated, wd_v[:, pl.ds(pl.multiple_of(p * group, LANES), group)])
        for a in range(ny):
            for zz in range(nz):
                at = (a * nz + zz) * cols
                piece = jnp.concatenate([out[:, at : at + cols], jnp.zeros((slots, LANES - cols), F32)], axis=1)
                osend[zz, :, rows_at((p * ny + a) * LANES, LANES)] = piece.astype(BF16)
        lanes = lanes_from(p)
        remote(
            osend.at[z_far, top, lanes], far_recv.at[0, :, lanes], far_send_sem, far_recv_sem.at[0, k], at_ring(z_next)
        ).start()
        remote(
            osend.at[z_far, low_half, lanes], far_recv.at[1, :, lanes], far_send_sem, far_recv_sem.at[1, k], at_ring(z_prev)
        ).start()
    for k in range(nx):
        lanes = lanes_from((x + k) % nx)
        remote(
            osend.at[z_next, low_half, lanes],
            near_recv.at[0, low_half, lanes],
            near_send_sem,
            near_recv_sem.at[0, k],
            at_ring(z_next),
        ).start()
        remote(
            osend.at[z_prev, top, lanes], near_recv.at[1, top, lanes], near_send_sem, near_recv_sem.at[1, k], at_ring(z_prev)
        ).start()
    for k in range(nx):
        lanes = lanes_from((x + k) % nx)
        drain(far_recv.at[0, :, lanes], far_recv_sem.at[0, k])
        near_send[0, :, lanes] = (osend[z_next, top, lanes].astype(F32) + far_recv[0, :, lanes].astype(F32)).astype(BF16)
        remote(
            near_send.at[0, :, lanes], near_recv.at[0, top, lanes], near_send_sem, near_recv_sem.at[2, k], at_ring(z_next)
        ).start()
        drain(far_recv.at[1, :, lanes], far_recv_sem.at[1, k])
        near_send[1, :, lanes] = (
            osend[z_prev, low_half, lanes].astype(F32) + far_recv[1, :, lanes].astype(F32)
        ).astype(BF16)
        remote(
            near_send.at[1, :, lanes],
            near_recv.at[1, low_half, lanes],
            near_send_sem,
            near_recv_sem.at[3, k],
            at_ring(z_prev),
        ).start()
    for k in range(nx):
        p = (x + k) % nx
        lanes = lanes_from(p)
        drain(near_recv.at[0, low_half, lanes], near_recv_sem.at[0, k])
        drain(near_recv.at[1, top, lanes], near_recv_sem.at[1, k])
        drain(near_recv.at[0, top, lanes], near_recv_sem.at[2, k])
        drain(near_recv.at[1, low_half, lanes], near_recv_sem.at[3, k])
        summed = osend[z, :, lanes].astype(F32) + near_recv[0, :, lanes].astype(F32)
        fin[:, lanes] = (summed + near_recv[1, :, lanes].astype(F32)).astype(BF16)
        for a in range(ny):
            for ds in range(side_n):
                ss = (side + ds) % side_n
                target = p * ny + (y + a) % ny
                src = fin.at[rows_at(ss * cap, cap), rows_at(target * LANES, LANES)]
                if k == 0 and a == 0 and ds == 0:
                    pltpu.make_async_copy(src, ret.at[home, :], ret_recv_sem).start()
                else:
                    to = {"side": ss, "dev": target * nz + z}
                    remote(src, ret.at[home, :], ret_send_sem, ret_recv_sem, to).start()

    drain(ret, ret_recv_sem)
    total = (ret[...].astype(F32) * wslot[...]).T
    high = total.astype(BF16)
    low = (total - high.astype(F32)).astype(BF16)
    routed = nn_dot(jnp.concatenate([high, low], axis=0), onehot[...])
    result = hid_t[...] + routed[0:LANES] + routed[LANES : 2 * LANES]
    out_ref[...] = result[0:cols]

    drain(wo_v.at[0 : nz - 1, pl.ds(0, cols), my_half], wo_send_sem)
    drain(vu_v.at[0 : (nx - 1) * (ny + 1), my_rows, :], vu_send_sem)
    drain(vu_v.at[:, my_rows, :], vu_swap_send_sem)
    for swap in wo_swaps:
        swap.wait_send()
    drain(ctx_send.at[0 : nz - 1], ctx_send_sem)
    drain(val_v.at[0 : 3 * (ny + 1) * blk], ag_send_sem)
    drain(part_send.at[0 : nz - 1], rs_send_sem)
    drain(ret.at[0 : (experts - 1) * cap], disp_send_sem)
    drain(ret.at[0 : (experts - 1) * cap], ret_send_sem)
    drain(rows.at[0:3], ring_send_sem)
    drain(far_recv, far_send_sem)
    drain(near_recv, near_send_sem)


def per_device(
    queries,
    latent_cache,
    cache_lengths,
    residual,
    value_up,
    out_proj,
    norm_gain,
    expert_ids,
    route_weights,
    w_gate,
    w_up,
    w_down,
):
    side_n = lax.axis_size("side")
    ndev = lax.axis_size("dev")
    nx = 4
    nz = nx
    plane = nx * nx
    tokens, cols = residual.shape
    reqs, heads, width = queries.shape
    length = latent_cache.shape[1]
    latent, vdim = value_up.shape[1:]
    units = w_gate.shape[1]
    experts = side_n * plane
    cap = 32
    blk = nz * reqs
    vmem = pl.BlockSpec(memory_space=pltpu.VMEM)
    hbm = pl.BlockSpec(memory_space=pl.ANY)
    dma = pltpu.SemaphoreType.DMA
    out = pl.pallas_call(
        functools.partial(layer_kernel, {"side": side_n, "x": nx, "z": nz}),
        out_shape=jax.ShapeDtypeStruct((cols, tokens), F32),
        in_specs=[hbm] * 12,
        out_specs=vmem,
        scratch_shapes=[
            pltpu.VMEM((reqs, heads, width), BF16),
            pltpu.SMEM((reqs,), jnp.int32),
            pltpu.VMEM((cols, tokens), BF16),
            pltpu.VMEM((1, cols), BF16),
            pltpu.VMEM((expert_ids.shape[1], tokens), jnp.int32),
            pltpu.VMEM((expert_ids.shape[1], tokens), F32),
            pltpu.VMEM((reqs, width, length), BF16),
            pltpu.VMEM((nz, plane, LANES, units), BF16),
            pltpu.VMEM((nz, plane, LANES, units), BF16),
            pltpu.VMEM((units, ndev * cols), BF16),
            pltpu.VMEM((nz, LANES, plane * LANES), BF16),
            pltpu.VMEM((plane, latent, vdim), BF16),
            pltpu.VMEM((latent // LANES, reqs * heads, LANES), F32),
            pltpu.VMEM((nz, plane * reqs, latent), BF16),
            pltpu.VMEM((nz, plane * reqs, latent), BF16),
            pltpu.VMEM((tokens, plane * LANES), BF16),
            pltpu.VMEM((nz, tokens, LANES), BF16),
            pltpu.VMEM((nz, tokens, LANES), BF16),
            pltpu.VMEM((tokens, LANES), F32),
            pltpu.VMEM((tokens, LANES), F32),
            pltpu.VMEM((tokens, LANES), F32),
            pltpu.VMEM((LANES, tokens), F32),
            pltpu.VMEM((experts, tokens), F32),
            pltpu.VMEM((experts, tokens), F32),
            pltpu.VMEM((experts * cap, tokens), BF16),
            pltpu.VMEM((experts * cap, LANES), F32),
            pltpu.VMEM((experts * cap, LANES), BF16),
            pltpu.VMEM((nz, side_n * cap, plane * LANES), BF16),
            pltpu.VMEM((nz, side_n * cap, plane * LANES), BF16),
            pltpu.VMEM((2, cap, plane * LANES), BF16),
            pltpu.VMEM((2, cap, plane * LANES), BF16),
            pltpu.VMEM((2, side_n * cap, plane * LANES), BF16),
            pltpu.VMEM((side_n * cap, plane * LANES), BF16),
            pltpu.VMEM((experts * cap, LANES), BF16),
            dma((reqs,)),
            dma((reqs,)),
            dma((5,)),
            dma((3, nz)),
            dma(()),
            dma(()),
            dma((nz - 1, 2)),
            dma(()),
            dma(()),
            dma((nx - 1,)),
            dma((nx - 1, nx)),
            dma(()),
            dma(()),
            dma((2,)),
            dma((2,)),
            dma(()),
            dma((nz - 1, reqs // 2)),
            dma(()),
            dma((3,)),
            dma((4, nx)),
            dma(()),
            dma((nz - 1, nx)),
            dma(()),
            dma((nx,)),
            dma(()),
            dma((4, nx)),
            dma(()),
            dma((2, nx)),
            dma(()),
            dma((4, nx)),
            dma(()),
            dma(()),
        ],
        compiler_params=pltpu.CompilerParams(
            collective_id=0, has_side_effects=True, vmem_limit_bytes=56 * 1024 * 1024
        ),
    )(
        queries,
        latent_cache.transpose(0, 2, 1),
        cache_lengths,
        residual.T,
        value_up,
        out_proj.T,
        norm_gain.reshape(1, cols),
        expert_ids.T,
        route_weights.T,
        w_gate.reshape(plane, nz, cols, units),
        w_up.reshape(plane, nz, cols, units),
        w_down,
    )
    return out.astype(BF16).T


def solution(mesh):
    placed = (
        P(("side", "dev"), None, None),
        P(("side", "dev"), None, None),
        P(("side", "dev")),
        P("side", "dev"),
        P("dev", None, None),
        P(None, "dev"),
        P("dev"),
        P("side", None),
        P("side", None),
        P(None, ("side", "dev")),
        P(None, ("side", "dev")),
        P(("side", "dev"), None),
    )
    return jax.shard_map(
        per_device, mesh=mesh, in_specs=placed, out_specs=P("side", "dev"), check_vma=False
    )
```

```python
import functools

import jax
import jax.numpy as jnp
from jax import lax
from jax.experimental import pallas as pl
from jax.experimental.pallas import tpu as pltpu
from jax.sharding import PartitionSpec as P

MESH = pl.DeviceIdType.MESH
LANES = 128
SCORE_SCALE = 192.0 ** (-0.5)
NORM_EPS = 1e-06
BF16 = jnp.bfloat16
F32 = jnp.float32


def nt_dot(a, b):
    return lax.dot_general(a, b, (((1,), (1,)), ((), ())), preferred_element_type=F32)


def nn_dot(a, b):
    return jnp.dot(a, b, preferred_element_type=F32)


def layer_kernel(
    dims,
    q_hbm,
    cache_ref,
    len_hbm,
    res_hbm,
    vu_ref,
    wo_ref,
    gain_hbm,
    ids_hbm,
    rw_hbm,
    wg_ref,
    wu_ref,
    wd_ref,
    out_ref,
    q_ref,
    len_ref,
    res_ref,
    gain_ref,
    ids_ref,
    rw_ref,
    out_v,
    cache_v,
    wg_v,
    wu_v,
    wd_v,
    wo_v,
    vu_v,
    ctx_f,
    ctx_send,
    ctx_recv,
    val_v,
    part_send,
    part_recv,
    part_own,
    res_v,
    hid_v,
    hid_t,
    pos_v,
    wte_v,
    onehot,
    wslot,
    disp,
    rows,
    osend,
    near_recv,
    fin,
    ret,
    ret_more,
    cache_sem,
    q_sem,
    small_sem,
    weight_sem,
    wo_sem,
    wo_send_sem,
    wo_recv_sem,
    vu_sem,
    vu_send_sem,
    vu1_sem,
    vu2_sem,
    vu_swap_send_sem,
    vu_swap_recv_sem,
    wo_swap_send_sem,
    wo_swap_recv_sem,
    ctx_send_sem,
    ctx_recv_sem,
    ag_send_sem,
    ag1_sem,
    ag2_sem,
    rs_send_sem,
    rs_recv_sem,
    disp_send_sem,
    disp_recv_sem,
    ring_send_sem,
    ring_recv_sem,
    near_send_sem,
    near_recv_sem,
    ret_send_sem,
    ret_recv_sem,
):
    side_n, nx, nz = dims["side"], dims["x"], dims["z"]
    ny = nx
    plane = nx * ny
    ndev = plane * nz
    reqs, heads, _ = q_ref.shape
    length = cache_ref.shape[2]
    latent = vu_ref.shape[1]
    vdim = vu_ref.shape[2]
    cols = res_ref.shape[0]
    tokens = res_ref.shape[1]
    blk = nz * reqs
    chunk = ny * blk
    half = plane // side_n
    experts = side_n * plane
    cap = onehot.shape[0] // experts
    full = ndev * cols
    side = lax.axis_index("side")
    dev = lax.axis_index("dev")
    x = dev // (ny * nz)
    y = (dev // nz) % ny
    z = dev % nz
    own_block = x * ny + y
    up = jnp.where(side == 0, x, y)
    uq = jnp.where(side == 0, y, x)
    twin = 1 - side

    def block_of(w, u):
        return jnp.where(side == 0, w * ny + u, u * ny + w)

    def at_plane(block):
        return {"side": side, "dev": block * nz + z}

    def at_ring(zz):
        return {"side": side, "dev": own_block * nz + zz}

    def remote(src, dst, send, recv, target):
        return pltpu.make_async_remote_copy(
            src_ref=src, dst_ref=dst, send_sem=send, recv_sem=recv, device_id=target, device_id_type=MESH
        )

    def drain(ref, sem):
        pltpu.make_async_copy(ref, ref, sem).wait()

    def rows_at(start, size):
        return pl.ds(pl.multiple_of(start, size), size)

    for zz in range(nz):
        wo_v[zz, cols:, :] = jnp.zeros((LANES - cols, plane * LANES), BF16)
    barrier = pltpu.get_barrier_semaphore()
    mate = {"side": twin, "dev": dev}
    friends = [mate]
    for k in range(1, nx):
        friends.append({"side": side, "dev": (((x + k) % nx) * ny + y) * nz + z})
        friends.append({"side": side, "dev": (x * ny + (y + k) % ny) * nz + z})
        friends.append({"side": side, "dev": own_block * nz + (z + k) % nz})
    for friend in friends:
        pl.semaphore_signal(barrier, inc=1, device_id=friend, device_id_type=MESH)

    half_lanes = half * LANES
    half_rows = latent // side_n
    my_half = pl.ds(pl.multiple_of(side * half_lanes, half_lanes), half_lanes)
    my_rows = rows_at(side * half_rows, half_rows)

    def wo_source(j, zz):
        return wo_ref.at[:, rows_at((j * nz + zz) * LANES, LANES)]

    def wo_place(zz, j):
        return wo_v.at[zz, pl.ds(0, cols), rows_at(j * LANES, LANES)]

    own_vu = pltpu.make_async_copy(vu_ref.at[0, my_rows, :], vu_v.at[own_block, my_rows, :], vu_sem)
    own_vu.start()
    len_copy = pltpu.make_async_copy(len_hbm, len_ref, small_sem.at[0])
    len_copy.start()
    q_copy = pltpu.make_async_copy(q_hbm, q_ref, q_sem)
    q_copy.start()
    for r in range(2):
        pltpu.make_async_copy(cache_ref.at[r], cache_v.at[r], cache_sem.at[r]).start()
    small_copies = [
        pltpu.make_async_copy(source, place, small_sem.at[n + 1])
        for n, (source, place) in enumerate(
            ((res_hbm, res_ref), (gain_hbm, gain_ref), (ids_hbm, ids_ref), (rw_hbm, rw_ref))
        )
    ]
    weight_copies = [pltpu.make_async_copy(wd_ref, wd_v, weight_sem.at[2])]
    for zz in range(nz):
        for n, (source, place) in enumerate(((wg_ref, wg_v), (wu_ref, wu_v))):
            weight_copies.append(
                pltpu.make_async_copy(source.at[:, zz], place.at[zz, :, pl.ds(0, cols), :], weight_sem.at[n])
            )

    place_no = lax.broadcasted_iota(jnp.int32, (1, length), 1)

    def attend(first):
        pair = (first, first + 1)
        for r in pair:
            pltpu.make_async_copy(cache_ref.at[r], cache_v.at[r], cache_sem.at[r]).wait()
        if first == 0:
            for r in range(2, reqs):
                pltpu.make_async_copy(cache_ref.at[r], cache_v.at[r], cache_sem.at[r]).start()
        scores = []
        for r in pair:
            outside = jnp.where(place_no < len_ref[r], 0.0, -1e30)
            scores.append(nn_dot(q_ref[r], cache_v[r]) * SCORE_SCALE + outside)
        for r, own in zip(pair, scores):
            weights = jnp.exp(own - jnp.max(own, axis=1, keepdims=True))
            weights = (weights * (1.0 / jnp.sum(weights, axis=1, keepdims=True))).astype(BF16)
            context = nt_dot(weights, cache_v[r, 0:latent, :])
            for b in range(latent // LANES):
                ctx_f[b, r * heads : (r + 1) * heads, :] = context[:, b * LANES : (b + 1) * LANES]

    pl.semaphore_wait(barrier, len(friends))
    for k in range(1, nx):
        remote(
            vu_ref.at[0, my_rows, :],
            vu_v.at[own_block, my_rows, :],
            vu_send_sem,
            vu1_sem.at[k - 1],
            at_plane(block_of(up, (uq + k) % ny)),
        ).start()
    cuts = (0, half // 4, half)

    def lanes_of(part):
        start = side * half_lanes + cuts[part] * LANES
        return pl.ds(pl.multiple_of(start, LANES), (cuts[part + 1] - cuts[part]) * LANES)

    def exchange_wo(part):
        for i in range(cuts[part], cuts[part + 1]):
            for k in range(1, nz):
                to = (z + k) % nz
                j = side * half + i
                remote(
                    wo_source(j, to), wo_place(z, j), wo_send_sem, wo_recv_sem.at[k - 1, part], at_ring(to)
                ).start()

    def swap_wo(part):
        for k in range(1, nz):
            drain(wo_v.at[(z + nz - k) % nz, pl.ds(0, cols), lanes_of(part)], wo_recv_sem.at[k - 1, part])
        piece = wo_v.at[:, :, lanes_of(part)]
        copy = remote(piece, piece, wo_swap_send_sem.at[part], wo_swap_recv_sem.at[part], mate)
        copy.start()
        return copy

    def forward_vu(a):
        block = block_of(up, (uq + ny - a) % ny)
        piece = vu_v.at[block, my_rows, :]
        if a > 0:
            drain(piece, vu1_sem.at[a - 1])
        for k in range(1, nx):
            to = at_plane(block_of((up + k) % nx, uq))
            source = piece if a > 0 else vu_ref.at[0, my_rows, :]
            remote(source, piece, vu_send_sem, vu2_sem.at[k - 1], to).start()

    exchange_wo(0)
    len_copy.wait()
    q_copy.wait()

    pairs = reqs // 2

    def send_contexts(g):
        for r in (2 * g, 2 * g + 1):
            for zz in range(nz):
                pieces = [
                    ctx_f[b, pl.ds(r * heads + zz, plane, stride=nz), :] for b in range(latent // LANES)
                ]
                ctx_send[zz, r * plane : (r + 1) * plane, :] = jnp.concatenate(pieces, axis=1).astype(BF16)
        at = pl.ds(2 * g * plane, 2 * plane)
        for k in range(1, nz):
            to = (z + k) % nz
            remote(
                ctx_send.at[to, at, :], ctx_recv.at[z, at, :], ctx_send_sem, ctx_recv_sem.at[k - 1], at_ring(to)
            ).start()

    for g in range(pairs):
        attend(2 * g)
        send_contexts(g)
        if g == 0:
            forward_vu(0)
            for i in range(half):
                j = side * half + i
                pltpu.make_async_copy(wo_source(j, z), wo_place(z, j), wo_sem).start()
        if g == 1:
            forward_vu(1)
            forward_vu(3)
        if g == 2:
            forward_vu(2)
            for copy in small_copies + weight_copies:
                copy.start()
    exchange_wo(1)
    ctx_recv[z] = ctx_send[z]

    def swap_vu(k):
        w = (up + nx - k) % nx
        if k == 0:
            own_vu.wait()
        else:
            drain(vu_v.at[0:ny, my_rows, :], vu2_sem.at[k - 1])
        for a in range(ny):
            block = block_of(w, (uq + ny - a) % ny)
            piece = vu_v.at[block, my_rows, :]
            remote(piece, piece, vu_swap_send_sem, vu_swap_recv_sem, mate).start()

    for k in (0, 1, 3, 2):
        swap_vu(k)
    drain(wo_v.at[z, pl.ds(0, cols), my_half], wo_sem)
    wo_swaps = [swap_wo(0)]

    for copy in small_copies:
        copy.wait()
    ids = ids_ref[...]
    rw = rw_ref[...]
    expert_no = lax.broadcasted_iota(jnp.int32, (experts, tokens), 0)
    chosen = jnp.zeros((experts, tokens), F32)
    wte = jnp.zeros((experts, tokens), F32)
    for k in range(ids.shape[0]):
        match = ids[k : k + 1, :] == expert_no
        chosen = jnp.where(match, 1.0, chosen)
        wte = wte + jnp.where(match, rw[k : k + 1, :], 0.0)
    before = lax.broadcasted_iota(jnp.int32, (tokens, tokens), 0) < lax.broadcasted_iota(
        jnp.int32, (tokens, tokens), 1
    )
    position = nn_dot(chosen.astype(BF16), jnp.where(before, 1.0, 0.0).astype(BF16))
    pos_v[...] = jnp.where(chosen > 0.0, position, -1.0)
    wte_v[...] = wte

    def fill(e, carry):
        slot = lax.broadcasted_iota(jnp.int32, (cap, tokens), 0).astype(F32)
        hit = pos_v[pl.ds(e, 1), :] == slot
        onehot[rows_at(e * cap, cap), :] = jnp.where(hit, 1.0, 0.0).astype(BF16)
        picked = jnp.sum(jnp.where(hit, wte_v[pl.ds(e, 1), :], 0.0), axis=1, keepdims=True)
        wslot[rows_at(e * cap, cap), :] = jnp.broadcast_to(picked, (cap, LANES))
        return carry

    res_t = jnp.concatenate(
        [res_ref[...].astype(F32), jnp.zeros((LANES - cols, tokens), F32)], axis=0
    )
    res_v[...] = res_t.T
    for zz in range(nz):
        for j in range(plane):
            wg_v[zz, j, cols:, :] = jnp.zeros((LANES - cols, wg_v.shape[3]), BF16)
            wu_v[zz, j, cols:, :] = jnp.zeros((LANES - cols, wu_v.shape[3]), BF16)
    part_recv[z] = jnp.zeros((tokens, LANES), BF16)

    lax.fori_loop(experts // 4, experts // 2, fill, 0)
    drain(vu_v.at[:, rows_at(twin * half_rows, half_rows), :], vu_swap_recv_sem)
    for k in range(1, nz):
        drain(ctx_recv.at[(z + nz - k) % nz], ctx_recv_sem.at[k - 1])
    my_block = rows_at(own_block * blk, blk)
    for zz in range(nz):
        for b in range(latent // LANES):
            ctx_f[b, zz * reqs * plane : (zz + 1) * reqs * plane, :] = ctx_recv[
                zz, :, b * LANES : (b + 1) * LANES
            ].astype(F32)
    for jp in range(plane // 2):
        lhs = [
            jnp.concatenate(
                [ctx_f[b, pl.ds(j, blk, stride=plane), :] for b in range(latent // LANES)], axis=1
            )
            for j in (2 * jp, 2 * jp + 1)
        ]
        rhs = jnp.concatenate([vu_v[2 * jp], vu_v[2 * jp + 1]], axis=1)
        both = nn_dot(jnp.concatenate(lhs, axis=0).astype(BF16), rhs)
        picked = jnp.concatenate([both[0:blk, 0:vdim], both[blk : 2 * blk, vdim : 2 * vdim]], axis=1)
        val_v[my_block, jp * 2 * vdim : (jp + 1) * 2 * vdim] = picked.astype(BF16)

    half_blk = blk // 2

    def block_rows(w, u, part=None):
        start = block_of(w, u) * blk
        if part is None:
            return val_v.at[rows_at(start, blk), :]
        return val_v.at[rows_at(start + part * half_blk, half_blk), :]

    ahead, behind = (up + 1) % nx, (up + nx - 1) % nx
    across = (up + 2) % nx
    u_ahead, u_behind, u_across = (uq + 1) % ny, (uq + ny - 1) % ny, (uq + 2) % ny

    def pass_u(piece, u, sem):
        remote(piece, piece, ag_send_sem, ag1_sem.at[sem], at_plane(block_of(up, u))).start()

    def pass_w(piece, forward, sem, a):
        to = at_plane(block_of(ahead if forward else behind, uq))
        remote(piece, piece, ag_send_sem, ag2_sem.at[sem, a], to).start()

    us = [uq, u_behind, u_ahead, u_across]
    mine = block_rows(up, uq)
    pass_u(mine, u_ahead, 0)
    pass_u(mine, u_behind, 1)
    pass_u(mine, u_across, 2)
    lax.fori_loop(0, experts // 4, fill, 0)
    pass_w(mine, True, 0, 0)
    pass_w(mine, False, 1, 0)
    for a in range(1, ny):
        piece = block_rows(up, us[a])
        drain(piece, ag1_sem.at[a - 1])
        pass_w(piece, True, 0, a)
        pass_w(piece, False, 1, a)
        if a == 2:
            wo_swaps.append(swap_wo(1))
        if a == 3:
            to = at_plane(block_of(across, uq))
            remote(piece, piece, ag_send_sem, ag2_sem.at[2, a], to).start()

    def hand_on(a):
        drain(block_rows(behind, us[a]), ag2_sem.at[0, a])
        pass_w(block_rows(behind, us[a], 0), True, 2, a)
        drain(block_rows(ahead, us[a]), ag2_sem.at[1, a])
        pass_w(block_rows(ahead, us[a], 1), False, 3, a)

    def project(k):
        w = (up, behind, ahead, across)[k]
        lhs = jnp.concatenate([val_v[rows_at(block_of(w, u) * blk, blk), :] for u in range(ny)], axis=0)
        at = rows_at(w * chunk, chunk)
        own = jnp.zeros((chunk, LANES), F32)
        for zz in range(nz):
            part = nt_dot(lhs, wo_v[zz])
            own = jnp.where(z == zz, part, own)
            part_send[zz, at, :] = part.astype(BF16)
        part_own[at, :] = own
        for kk in range(1, nz):
            to = (z + kk) % nz
            remote(
                part_send.at[to, at, :], part_recv.at[z, at, :], rs_send_sem, rs_recv_sem.at[kk - 1], at_ring(to)
            ).start()

    hand_on(0)
    for swap in wo_swaps:
        swap.wait_recv()
    project(0)
    lax.fori_loop(experts // 2, 3 * experts // 4, fill, 0)
    hand_on(1)
    hand_on(2)
    for sem, w in ((0, behind), (1, ahead)):
        drain(block_rows(w, us[3]), ag2_sem.at[sem, 3])
    project(1)
    project(2)
    lax.fori_loop(3 * experts // 4, experts, fill, 0)
    for a in range(ny - 1):
        drain(block_rows(across, us[a], 0), ag2_sem.at[2, a])
        drain(block_rows(across, us[a], 1), ag2_sem.at[3, a])
    drain(block_rows(across, us[3]), ag2_sem.at[2, 3])
    project(3)
    for kk in range(1, nz):
        drain(part_recv.at[(z + nz - kk) % nz], rs_recv_sem.at[kk - 1])
    for w in range(nx):
        for u in range(ny):
            here = (w * ny + u) * blk
            total = part_own[here : here + blk, :]
            for zz in range(nz):
                total = total + part_recv[zz, here : here + blk, :].astype(F32)
            there = rows_at(block_of(w, u) * blk, blk)
            hid_v[there, :] = total + res_v[there, :]

    hidden = hid_v[...]
    squares = jnp.sum(hidden * hidden, axis=1, keepdims=True)
    high = squares.astype(BF16).astype(F32)
    middle = (squares - high).astype(BF16).astype(F32)
    low = squares - high - middle
    lane = lax.broadcasted_iota(jnp.int32, (tokens, LANES), 1)
    gain = jnp.concatenate([gain_ref[...].astype(F32), jnp.zeros((1, LANES - cols), F32)], axis=1)
    extended = hidden * gain
    extended = jnp.where(lane == cols, high, extended)
    extended = jnp.where(lane == cols + 1, middle, extended)
    extended = jnp.where(lane == cols + 2, low, extended)
    part = cap // 2
    disp[...] = nn_dot(onehot[...], extended.astype(BF16)).astype(BF16).reshape(experts, 2, part, LANES)

    my_slots = rows_at(side * part, part)
    my_lanes = rows_at(own_block * LANES, LANES)
    own_expert = side * plane + own_block
    z_next, z_prev, z_far = (z + 1) % nz, (z + nz - 1) % nz, (z + 2) % nz

    def dispatch_halves(expert, ss, target, dx):
        for h, to in ((0, z_next), (1, z_prev)):
            remote(
                disp.at[expert, h],
                rows.at[z, h, my_slots, my_lanes],
                disp_send_sem.at[1],
                disp_recv_sem.at[1 + h, dx],
                {"side": ss, "dev": target * nz + to},
            ).start()

    def dispatch(i, carry):
        ss = (side + i) % side_n
        sy = (y + (i // side_n) % ny) % ny
        turn = i // (side_n * ny)
        dx = jnp.where(turn == 0, 0, jnp.where(turn == 1, 2, jnp.where(turn == 2, 1, 3)))
        target = ((x + dx) % nx) * ny + sy
        expert = ss * plane + target
        remote(
            disp.at[expert],
            rows.at[z, :, my_slots, my_lanes],
            disp_send_sem.at[0],
            disp_recv_sem.at[0, dx],
            {"side": ss, "dev": target * nz + z},
        ).start()
        dispatch_halves(expert, ss, target, dx)
        return carry

    pltpu.make_async_copy(disp.at[own_expert], rows.at[z, :, my_slots, my_lanes], disp_recv_sem.at[0, 0]).start()
    dispatch_halves(own_expert, side, own_block, 0)
    lax.fori_loop(1, experts, dispatch, 0)
    hid_t[...] = hidden.T

    width = ny * LANES
    slots = side_n * cap
    units = wg_v.shape[3]

    def lanes_from(p):
        return pl.ds(pl.multiple_of(p * width, width), width)

    def piece_of(zz, dx, h=None):
        lanes = lanes_from((x + nx - dx) % nx)
        if h is None:
            return rows.at[zz, :, :, lanes]
        return rows.at[zz, h, :, lanes]

    def along(piece, to, n, dx):
        remote(piece, piece, ring_send_sem, ring_recv_sem.at[n], at_ring(to)).start()

    for dx in (0, 2, 1, 3):
        drain(piece_of(z, dx), disp_recv_sem.at[0, dx])
        along(piece_of(z, dx, 1), z_next, 0, dx)
        along(piece_of(z, dx, 0), z_prev, 1, dx)
        drain(piece_of(z_prev, dx, 0), disp_recv_sem.at[1, dx])
        along(piece_of(z_prev, dx, 0), z_next, 2, dx)
        drain(piece_of(z_next, dx, 1), disp_recv_sem.at[2, dx])
        along(piece_of(z_next, dx, 1), z_prev, 3, dx)
    weight_copies[0].wait()
    drain(wg_v.at[:, :, pl.ds(0, cols), :], weight_sem.at[0])
    drain(wu_v.at[:, :, pl.ds(0, cols), :], weight_sem.at[1])
    gate = jnp.zeros((slots, units), F32)
    upward = jnp.zeros((slots, units), F32)
    marks = jnp.zeros((slots, LANES), F32)

    def take(zz, gate, upward, marks):
        lhs = rows[zz].reshape(slots, plane * LANES)
        gate = gate + nn_dot(lhs, wg_v[zz].reshape(plane * LANES, units))
        upward = upward + nn_dot(lhs, wu_v[zz].reshape(plane * LANES, units))
        for j in range(plane):
            marks = marks + lhs[:, j * LANES : (j + 1) * LANES].astype(F32)
        return gate, upward, marks

    gate, upward, marks = take(z, gate, upward, marks)
    drain(rows.at[z_prev, 1], ring_recv_sem.at[0])
    gate, upward, marks = take(z_prev, gate, upward, marks)
    drain(rows.at[z_next, 0], ring_recv_sem.at[1])
    gate, upward, marks = take(z_next, gate, upward, marks)
    drain(rows.at[z_far, 0], ring_recv_sem.at[2])
    drain(rows.at[z_far, 1], ring_recv_sem.at[3])
    gate, upward, marks = take(z_far, gate, upward, marks)
    mark_lane = lax.broadcasted_iota(jnp.int32, (slots, LANES), 1)
    marks = jnp.where((mark_lane >= cols) & (mark_lane < cols + 3), marks, 0.0)
    scale = lax.rsqrt(jnp.sum(marks, axis=1, keepdims=True) / full + NORM_EPS)
    gate = gate * scale
    activated = (gate / (1.0 + jnp.exp(-gate)) * (upward * scale)).astype(BF16)

    group = ny * nz * cols
    turns = (2, 1, 3, 0)
    for k in turns:
        p = (x + k) % nx
        out = nn_dot(activated, wd_v[:, pl.ds(pl.multiple_of(p * group, LANES), group)])
        for a in range(ny):
            for zz in range(nz):
                at = (a * nz + zz) * cols
                piece = jnp.concatenate([out[:, at : at + cols], jnp.zeros((slots, LANES - cols), F32)], axis=1)
                osend[zz, :, :, rows_at((p * ny + a) * LANES, LANES)] = piece.astype(BF16).reshape(
                    2, slots // 2, LANES
                )
        lanes = lanes_from(p)
        for n, (source, h, to) in enumerate(
            ((z_next, 0, z_next), (z_prev, 1, z_prev), (z_far, 0, z_prev), (z_far, 1, z_next))
        ):
            remote(
                osend.at[source, h, :, lanes], near_recv.at[n, :, lanes], near_send_sem, near_recv_sem.at[n, k], at_ring(to)
            ).start()
    for k in turns:
        p = (x + k) % nx
        lanes = lanes_from(p)
        for n, (held, h, place) in enumerate(((z, 0, 0), (z, 1, 1), (z_prev, 0, 2), (z_next, 1, 3))):
            drain(near_recv.at[n, :, lanes], near_recv_sem.at[n, k])
            summed = osend[held, h, :, lanes].astype(F32) + near_recv[n, :, lanes].astype(F32)
            fin[place, :, lanes] = summed.astype(BF16)
        for a in range(ny):
            target = p * ny + (y + a) % ny
            at = rows_at(target * LANES, LANES)
            for ds in range(side_n):
                ss = (side + ds) % side_n
                its = rows_at(ss * part, part)
                src = fin.at[0:2, its, at]
                if k == 0 and a == 0 and ds == 0:
                    pltpu.make_async_copy(src, ret.at[own_expert], ret_recv_sem.at[0]).start()
                else:
                    to = {"side": ss, "dev": target * nz + z}
                    remote(src, ret.at[own_expert], ret_send_sem.at[0], ret_recv_sem.at[0], to).start()
                for h, zz in ((0, z_prev), (1, z_next)):
                    remote(
                        fin.at[2 + h, its, at],
                        ret_more.at[own_expert, h],
                        ret_send_sem.at[1],
                        ret_recv_sem.at[1],
                        {"side": ss, "dev": target * nz + zz},
                    ).start()

    drain(ret, ret_recv_sem.at[0])
    drain(ret_more, ret_recv_sem.at[1])
    total = (ret[...].astype(F32) + ret_more[...].astype(F32)).reshape(experts * cap, LANES)
    total = (total * wslot[...]).T
    high = total.astype(BF16)
    low = (total - high.astype(F32)).astype(BF16)
    routed = nn_dot(jnp.concatenate([high, low], axis=0), onehot[...])
    result = hid_t[...] + routed[0:LANES] + routed[LANES : 2 * LANES]
    out_v[...] = result[0:cols]
    out_copy = pltpu.make_async_copy(out_v, out_ref, small_sem.at[5])
    out_copy.start()

    drain(wo_v.at[0 : nz - 1, pl.ds(0, cols), my_half], wo_send_sem)
    drain(vu_v.at[0 : (nx - 1) * (ny + 1), my_rows, :], vu_send_sem)
    drain(vu_v.at[:, my_rows, :], vu_swap_send_sem)
    for swap in wo_swaps:
        swap.wait_send()
    drain(ctx_send.at[0 : nz - 1], ctx_send_sem)
    drain(val_v.at[0 : 3 * (ny + 1) * blk], ag_send_sem)
    drain(part_send.at[0 : nz - 1], rs_send_sem)
    drain(disp.at[0 : experts - 1], disp_send_sem.at[0])
    drain(disp, disp_send_sem.at[1])
    drain(ret.at[0 : experts - 1], ret_send_sem.at[0])
    drain(ret_more, ret_send_sem.at[1])
    drain(rows.at[0:2], ring_send_sem)
    drain(near_recv, near_send_sem)
    out_copy.wait()


def per_device(
    queries,
    latent_cache,
    cache_lengths,
    residual,
    value_up,
    out_proj,
    norm_gain,
    expert_ids,
    route_weights,
    w_gate,
    w_up,
    w_down,
):
    side_n = lax.axis_size("side")
    ndev = lax.axis_size("dev")
    nx = 4
    nz = nx
    plane = nx * nx
    tokens, cols = residual.shape
    reqs, heads, width = queries.shape
    length = latent_cache.shape[1]
    latent, vdim = value_up.shape[1:]
    units = w_gate.shape[1]
    experts = side_n * plane
    cap = 32
    blk = nz * reqs
    hbm = pl.BlockSpec(memory_space=pl.ANY)
    dma = pltpu.SemaphoreType.DMA
    out = pl.pallas_call(
        functools.partial(layer_kernel, {"side": side_n, "x": nx, "z": nz}),
        out_shape=jax.ShapeDtypeStruct((cols, tokens), F32),
        in_specs=[hbm] * 12,
        out_specs=hbm,
        scratch_shapes=[
            pltpu.VMEM((reqs, heads, width), BF16),
            pltpu.SMEM((reqs,), jnp.int32),
            pltpu.VMEM((cols, tokens), BF16),
            pltpu.VMEM((1, cols), BF16),
            pltpu.VMEM((expert_ids.shape[1], tokens), jnp.int32),
            pltpu.VMEM((expert_ids.shape[1], tokens), F32),
            pltpu.VMEM((cols, tokens), F32),
            pltpu.VMEM((reqs, width, length), BF16),
            pltpu.VMEM((nz, plane, LANES, units), BF16),
            pltpu.VMEM((nz, plane, LANES, units), BF16),
            pltpu.VMEM((units, ndev * cols), BF16),
            pltpu.VMEM((nz, LANES, plane * LANES), BF16),
            pltpu.VMEM((plane, latent, vdim), BF16),
            pltpu.VMEM((latent // LANES, reqs * heads, LANES), F32),
            pltpu.VMEM((nz, plane * reqs, latent), BF16),
            pltpu.VMEM((nz, plane * reqs, latent), BF16),
            pltpu.VMEM((tokens, plane * LANES), BF16),
            pltpu.VMEM((nz, tokens, LANES), BF16),
            pltpu.VMEM((nz, tokens, LANES), BF16),
            pltpu.VMEM((tokens, LANES), F32),
            pltpu.VMEM((tokens, LANES), F32),
            pltpu.VMEM((tokens, LANES), F32),
            pltpu.VMEM((LANES, tokens), F32),
            pltpu.VMEM((experts, tokens), F32),
            pltpu.VMEM((experts, tokens), F32),
            pltpu.VMEM((experts * cap, tokens), BF16),
            pltpu.VMEM((experts * cap, LANES), F32),
            pltpu.VMEM((experts, 2, cap // 2, LANES), BF16),
            pltpu.VMEM((nz, 2, side_n * cap // 2, plane * LANES), BF16),
            pltpu.VMEM((nz, 2, side_n * cap // 2, plane * LANES), BF16),
            pltpu.VMEM((4, side_n * cap // 2, plane * LANES), BF16),
            pltpu.VMEM((4, side_n * cap // 2, plane * LANES), BF16),
            pltpu.VMEM((experts, 2, cap // 2, LANES), BF16),
            pltpu.VMEM((experts, 2, cap // 2, LANES), BF16),
        ]
        + [
            dma((reqs,)),
            dma(()),
            dma((6,)),
            dma((3,)),
            dma(()),
            dma(()),
            dma((nz - 1, 2)),
            dma(()),
            dma(()),
            dma((nx - 1,)),
            dma((nx - 1,)),
            dma(()),
            dma(()),
            dma((2,)),
            dma((2,)),
            dma(()),
            dma((nz - 1,)),
            dma(()),
            dma((3,)),
            dma((4, nx)),
            dma(()),
            dma((nz - 1,)),
            dma((2,)),
            dma((3, nx)),
            dma(()),
            dma((4,)),
            dma(()),
            dma((4, nx)),
            dma((2,)),
            dma((2,)),
        ],
        compiler_params=pltpu.CompilerParams(
            collective_id=0, has_side_effects=True, vmem_limit_bytes=56 * 1024 * 1024
        ),
    )(
        queries,
        latent_cache.transpose(0, 2, 1),
        cache_lengths,
        residual.T,
        value_up,
        out_proj.T,
        norm_gain.reshape(1, cols),
        expert_ids.T,
        route_weights.T,
        w_gate.reshape(plane, nz, cols, units),
        w_up.reshape(plane, nz, cols, units),
        w_down,
    )
    return out.astype(BF16).T


def solution(mesh):
    placed = (
        P(("side", "dev"), None, None),
        P(("side", "dev"), None, None),
        P(("side", "dev")),
        P("side", "dev"),
        P("dev", None, None),
        P(None, "dev"),
        P("dev"),
        P("side", None),
        P("side", None),
        P(None, ("side", "dev")),
        P(None, ("side", "dev")),
        P(("side", "dev"), None),
    )
    return jax.shard_map(
        per_device, mesh=mesh, in_specs=placed, out_specs=P("side", "dev"), check_vma=False
    )
```

```python
import functools

import jax
import jax.numpy as jnp
from jax import lax
from jax.experimental import pallas as pl
from jax.experimental.pallas import tpu as pltpu
from jax.sharding import PartitionSpec as P

MESH = pl.DeviceIdType.MESH
LANES = 128
SCORE_SCALE = 192.0 ** (-0.5)
NORM_EPS = 1e-06
BF16 = jnp.bfloat16
F32 = jnp.float32


def nt_dot(a, b):
    return lax.dot_general(a, b, (((1,), (1,)), ((), ())), preferred_element_type=F32)


def nn_dot(a, b):
    return jnp.dot(a, b, preferred_element_type=F32)


def layer_kernel(
    dims,
    q_hbm,
    cache_ref,
    len_hbm,
    res_hbm,
    vu_ref,
    wo_ref,
    gain_hbm,
    ids_hbm,
    rw_hbm,
    wg_ref,
    wu_ref,
    wd_ref,
    out_ref,
    q_ref,
    len_ref,
    res_ref,
    gain_ref,
    ids_ref,
    rw_ref,
    out_v,
    cache_v,
    wg_v,
    wu_v,
    wd_v,
    wo_v,
    vu_v,
    ctx_f,
    ctx_send,
    ctx_recv,
    val_v,
    part_send,
    part_recv,
    part_own,
    res_v,
    hid_v,
    hid_t,
    pos_v,
    wte_v,
    onehot,
    wslot,
    disp,
    rows,
    osend,
    near_recv,
    fin,
    ret,
    ret_more,
    cache_sem,
    q_sem,
    small_sem,
    weight_sem,
    wo_sem,
    wo_send_sem,
    wo_recv_sem,
    vu_sem,
    vu_send_sem,
    vu1_sem,
    vu2_sem,
    vu_swap_send_sem,
    vu_swap_recv_sem,
    wo_swap_send_sem,
    wo_swap_recv_sem,
    ctx_send_sem,
    ctx_recv_sem,
    ag_send_sem,
    ag1_sem,
    ag2_sem,
    rs_send_sem,
    rs_recv_sem,
    disp_send_sem,
    disp_recv_sem,
    ring_send_sem,
    ring_recv_sem,
    near_send_sem,
    near_recv_sem,
    ret_send_sem,
    ret_recv_sem,
):
    side_n, nx, nz = dims["side"], dims["x"], dims["z"]
    ny = nx
    plane = nx * ny
    ndev = plane * nz
    reqs, heads, _ = q_ref.shape
    length = cache_ref.shape[2]
    latent = vu_ref.shape[1]
    vdim = vu_ref.shape[2]
    cols = res_ref.shape[0]
    tokens = res_ref.shape[1]
    blk = nz * reqs
    chunk = ny * blk
    half = plane // side_n
    experts = side_n * plane
    cap = onehot.shape[0] // experts
    full = ndev * cols
    side = lax.axis_index("side")
    dev = lax.axis_index("dev")
    x = dev // (ny * nz)
    y = (dev // nz) % ny
    z = dev % nz
    own_block = x * ny + y
    up = jnp.where(side == 0, x, y)
    uq = jnp.where(side == 0, y, x)
    twin = 1 - side

    def block_of(w, u):
        return jnp.where(side == 0, w * ny + u, u * ny + w)

    def at_plane(block):
        return {"side": side, "dev": block * nz + z}

    def at_ring(zz):
        return {"side": side, "dev": own_block * nz + zz}

    def remote(src, dst, send, recv, target):
        return pltpu.make_async_remote_copy(
            src_ref=src, dst_ref=dst, send_sem=send, recv_sem=recv, device_id=target, device_id_type=MESH
        )

    def drain(ref, sem):
        pltpu.make_async_copy(ref, ref, sem).wait()

    def rows_at(start, size):
        return pl.ds(pl.multiple_of(start, size), size)

    for zz in range(nz):
        wo_v[zz, cols:, :] = jnp.zeros((LANES - cols, plane * LANES), BF16)
    barrier = pltpu.get_barrier_semaphore()
    mate = {"side": twin, "dev": dev}
    friends = [mate]
    for k in range(1, nx):
        friends.append({"side": side, "dev": (((x + k) % nx) * ny + y) * nz + z})
        friends.append({"side": side, "dev": (x * ny + (y + k) % ny) * nz + z})
        friends.append({"side": side, "dev": own_block * nz + (z + k) % nz})
    for friend in friends:
        pl.semaphore_signal(barrier, inc=1, device_id=friend, device_id_type=MESH)

    half_lanes = half * LANES
    half_rows = latent // side_n
    my_half = pl.ds(pl.multiple_of(side * half_lanes, half_lanes), half_lanes)
    my_rows = rows_at(side * half_rows, half_rows)

    def wo_source(j, zz):
        return wo_ref.at[:, rows_at((j * nz + zz) * LANES, LANES)]

    def wo_place(zz, j):
        return wo_v.at[zz, pl.ds(0, cols), rows_at(j * LANES, LANES)]

    own_vu = pltpu.make_async_copy(vu_ref.at[0, my_rows, :], vu_v.at[own_block, my_rows, :], vu_sem)
    own_vu.start()
    len_copy = pltpu.make_async_copy(len_hbm, len_ref, small_sem.at[0])
    len_copy.start()
    q_copy = pltpu.make_async_copy(q_hbm, q_ref, q_sem)
    q_copy.start()
    for r in range(2):
        pltpu.make_async_copy(cache_ref.at[r], cache_v.at[r], cache_sem.at[r]).start()
    small_copies = [
        pltpu.make_async_copy(source, place, small_sem.at[n + 1])
        for n, (source, place) in enumerate(
            ((res_hbm, res_ref), (gain_hbm, gain_ref), (ids_hbm, ids_ref), (rw_hbm, rw_ref))
        )
    ]
    weight_copies = [pltpu.make_async_copy(wd_ref, wd_v, weight_sem.at[2])]
    for zz in range(nz):
        for n, (source, place) in enumerate(((wg_ref, wg_v), (wu_ref, wu_v))):
            weight_copies.append(
                pltpu.make_async_copy(source.at[:, zz], place.at[zz, :, pl.ds(0, cols), :], weight_sem.at[n])
            )

    place_no = lax.broadcasted_iota(jnp.int32, (1, length), 1)

    def attend(first):
        pair = (first, first + 1)
        for r in pair:
            pltpu.make_async_copy(cache_ref.at[r], cache_v.at[r], cache_sem.at[r]).wait()
        if first == 0:
            for r in range(2, reqs):
                pltpu.make_async_copy(cache_ref.at[r], cache_v.at[r], cache_sem.at[r]).start()
        scores = []
        for r in pair:
            outside = jnp.where(place_no < len_ref[r], 0.0, -1e30)
            scores.append(nn_dot(q_ref[r], cache_v[r]) * SCORE_SCALE + outside)
        for r, own in zip(pair, scores):
            weights = jnp.exp(own - jnp.max(own, axis=1, keepdims=True))
            weights = (weights * (1.0 / jnp.sum(weights, axis=1, keepdims=True))).astype(BF16)
            context = nt_dot(weights, cache_v[r, 0:latent, :])
            for b in range(latent // LANES):
                ctx_f[b, r * heads : (r + 1) * heads, :] = context[:, b * LANES : (b + 1) * LANES]

    pl.semaphore_wait(barrier, len(friends))
    for k in (1, 3, 2):
        remote(
            vu_ref.at[0, my_rows, :],
            vu_v.at[own_block, my_rows, :],
            vu_send_sem,
            vu1_sem.at[k - 1],
            at_plane(block_of(up, (uq + k) % ny)),
        ).start()
    cuts = (0, half // 4, half)

    def lanes_of(part):
        start = side * half_lanes + cuts[part] * LANES
        return pl.ds(pl.multiple_of(start, LANES), (cuts[part + 1] - cuts[part]) * LANES)

    def exchange_wo(part):
        for i in range(cuts[part], cuts[part + 1]):
            for k in range(1, nz):
                to = (z + k) % nz
                j = side * half + i
                remote(
                    wo_source(j, to), wo_place(z, j), wo_send_sem, wo_recv_sem.at[k - 1, part], at_ring(to)
                ).start()

    def swap_wo(part):
        for k in range(1, nz):
            drain(wo_v.at[(z + nz - k) % nz, pl.ds(0, cols), lanes_of(part)], wo_recv_sem.at[k - 1, part])
        piece = wo_v.at[:, :, lanes_of(part)]
        copy = remote(piece, piece, wo_swap_send_sem.at[part], wo_swap_recv_sem.at[part], mate)
        copy.start()
        return copy

    def forward_vu(a):
        block = block_of(up, (uq + ny - a) % ny)
        piece = vu_v.at[block, my_rows, :]
        if a > 0:
            drain(piece, vu1_sem.at[a - 1])
        for k in (1, 3, 2):
            to = at_plane(block_of((up + k) % nx, uq))
            source = piece if a > 0 else vu_ref.at[0, my_rows, :]
            remote(source, piece, vu_send_sem, vu2_sem.at[k - 1], to).start()

    exchange_wo(0)
    len_copy.wait()
    q_copy.wait()

    pairs = reqs // 2

    def send_contexts(g):
        for r in (2 * g, 2 * g + 1):
            for zz in range(nz):
                pieces = [
                    ctx_f[b, pl.ds(r * heads + zz, plane, stride=nz), :] for b in range(latent // LANES)
                ]
                ctx_send[zz, r * plane : (r + 1) * plane, :] = jnp.concatenate(pieces, axis=1).astype(BF16)
        at = pl.ds(2 * g * plane, 2 * plane)
        for k in (2, 1, 3):
            to = (z + k) % nz
            remote(
                ctx_send.at[to, at, :], ctx_recv.at[z, at, :], ctx_send_sem, ctx_recv_sem.at[k - 1], at_ring(to)
            ).start()

    for g in range(pairs):
        attend(2 * g)
        send_contexts(g)
        if g == 0:
            forward_vu(0)
            for i in range(half):
                j = side * half + i
                pltpu.make_async_copy(wo_source(j, z), wo_place(z, j), wo_sem).start()
        if g == 1:
            forward_vu(1)
            forward_vu(3)
        if g == 2:
            forward_vu(2)
            for copy in small_copies + weight_copies:
                copy.start()
    exchange_wo(1)
    ctx_recv[z] = ctx_send[z]

    def swap_vu(k):
        w = (up + nx - k) % nx
        if k == 0:
            own_vu.wait()
        else:
            drain(vu_v.at[0:ny, my_rows, :], vu2_sem.at[k - 1])
        for a in range(ny):
            block = block_of(w, (uq + ny - a) % ny)
            piece = vu_v.at[block, my_rows, :]
            remote(piece, piece, vu_swap_send_sem, vu_swap_recv_sem, mate).start()

    for k in (0, 1, 3, 2):
        swap_vu(k)
    drain(wo_v.at[z, pl.ds(0, cols), my_half], wo_sem)
    wo_swaps = [swap_wo(0)]

    for copy in small_copies:
        copy.wait()
    ids = ids_ref[...]
    rw = rw_ref[...]
    expert_no = lax.broadcasted_iota(jnp.int32, (experts, tokens), 0)
    chosen = jnp.zeros((experts, tokens), F32)
    wte = jnp.zeros((experts, tokens), F32)
    for k in range(ids.shape[0]):
        match = ids[k : k + 1, :] == expert_no
        chosen = jnp.where(match, 1.0, chosen)
        wte = wte + jnp.where(match, rw[k : k + 1, :], 0.0)
    before = lax.broadcasted_iota(jnp.int32, (tokens, tokens), 0) < lax.broadcasted_iota(
        jnp.int32, (tokens, tokens), 1
    )
    position = nn_dot(chosen.astype(BF16), jnp.where(before, 1.0, 0.0).astype(BF16))
    pos_v[...] = jnp.where(chosen > 0.0, position, -1.0)
    wte_v[...] = wte

    def fill(e, carry):
        slot = lax.broadcasted_iota(jnp.int32, (cap, tokens), 0).astype(F32)
        hit = pos_v[pl.ds(e, 1), :] == slot
        onehot[rows_at(e * cap, cap), :] = jnp.where(hit, 1.0, 0.0).astype(BF16)
        picked = jnp.sum(jnp.where(hit, wte_v[pl.ds(e, 1), :], 0.0), axis=1, keepdims=True)
        wslot[rows_at(e * cap, cap), :] = jnp.broadcast_to(picked, (cap, LANES))
        return carry

    res_t = jnp.concatenate(
        [res_ref[...].astype(F32), jnp.zeros((LANES - cols, tokens), F32)], axis=0
    )
    res_v[...] = res_t.T
    for zz in range(nz):
        for j in range(plane):
            wg_v[zz, j, cols:, :] = jnp.zeros((LANES - cols, wg_v.shape[3]), BF16)
            wu_v[zz, j, cols:, :] = jnp.zeros((LANES - cols, wu_v.shape[3]), BF16)
    part_recv[z] = jnp.zeros((tokens, LANES), BF16)

    lax.fori_loop(0, experts // 4, fill, 0)
    drain(vu_v.at[:, rows_at(twin * half_rows, half_rows), :], vu_swap_recv_sem)
    for k in range(1, nz):
        drain(ctx_recv.at[(z + nz - k) % nz], ctx_recv_sem.at[k - 1])
    my_block = rows_at(own_block * blk, blk)
    for zz in range(nz):
        for b in range(latent // LANES):
            ctx_f[b, zz * reqs * plane : (zz + 1) * reqs * plane, :] = ctx_recv[
                zz, :, b * LANES : (b + 1) * LANES
            ].astype(F32)
    for jp in range(plane // 2):
        lhs = [
            jnp.concatenate(
                [ctx_f[b, pl.ds(j, blk, stride=plane), :] for b in range(latent // LANES)], axis=1
            )
            for j in (2 * jp, 2 * jp + 1)
        ]
        rhs = jnp.concatenate([vu_v[2 * jp], vu_v[2 * jp + 1]], axis=1)
        both = nn_dot(jnp.concatenate(lhs, axis=0).astype(BF16), rhs)
        picked = jnp.concatenate([both[0:blk, 0:vdim], both[blk : 2 * blk, vdim : 2 * vdim]], axis=1)
        val_v[my_block, jp * 2 * vdim : (jp + 1) * 2 * vdim] = picked.astype(BF16)

    half_blk = blk // 2

    def block_rows(w, u, part=None):
        start = block_of(w, u) * blk
        if part is None:
            return val_v.at[rows_at(start, blk), :]
        return val_v.at[rows_at(start + part * half_blk, half_blk), :]

    ahead, behind = (up + 1) % nx, (up + nx - 1) % nx
    across = (up + 2) % nx
    u_ahead, u_behind, u_across = (uq + 1) % ny, (uq + ny - 1) % ny, (uq + 2) % ny

    def pass_u(piece, u, sem):
        remote(piece, piece, ag_send_sem, ag1_sem.at[sem], at_plane(block_of(up, u))).start()

    def pass_w(piece, forward, sem, a):
        to = at_plane(block_of(ahead if forward else behind, uq))
        remote(piece, piece, ag_send_sem, ag2_sem.at[sem, a], to).start()

    us = [uq, u_behind, u_ahead, u_across]
    mine = block_rows(up, uq)
    pass_u(mine, u_ahead, 0)
    pass_u(mine, u_behind, 1)
    lax.fori_loop(experts // 4, experts // 2, fill, 0)
    pass_u(mine, u_across, 2)
    lax.fori_loop(experts // 2, experts, fill, 0)
    pass_w(mine, True, 0, 0)
    pass_w(mine, False, 1, 0)
    for a in range(1, ny):
        piece = block_rows(up, us[a])
        drain(piece, ag1_sem.at[a - 1])
        pass_w(piece, True, 0, a)
        pass_w(piece, False, 1, a)
        if a == 2:
            wo_swaps.append(swap_wo(1))
        if a == 3:
            to = at_plane(block_of(across, uq))
            remote(piece, piece, ag_send_sem, ag2_sem.at[2, a], to).start()

    def hand_on(a):
        drain(block_rows(behind, us[a]), ag2_sem.at[0, a])
        pass_w(block_rows(behind, us[a], 0), True, 2, a)
        drain(block_rows(ahead, us[a]), ag2_sem.at[1, a])
        pass_w(block_rows(ahead, us[a], 1), False, 3, a)

    def project(k):
        w = (up, behind, ahead, across)[k]
        lhs = jnp.concatenate([val_v[rows_at(block_of(w, u) * blk, blk), :] for u in range(ny)], axis=0)
        at = rows_at(w * chunk, chunk)
        own = jnp.zeros((chunk, LANES), F32)
        for zz in range(nz):
            part = nt_dot(lhs, wo_v[zz])
            own = jnp.where(z == zz, part, own)
            part_send[zz, at, :] = part.astype(BF16)
        part_own[at, :] = own
        for kk in (2, 1, 3):
            to = (z + kk) % nz
            remote(
                part_send.at[to, at, :], part_recv.at[z, at, :], rs_send_sem, rs_recv_sem.at[kk - 1], at_ring(to)
            ).start()

    hand_on(0)
    for swap in wo_swaps:
        swap.wait_recv()
    project(0)
    hand_on(1)
    hand_on(2)
    for sem, w in ((0, behind), (1, ahead)):
        drain(block_rows(w, us[3]), ag2_sem.at[sem, 3])
    project(1)
    project(2)
    for a in range(ny - 1):
        drain(block_rows(across, us[a], 0), ag2_sem.at[2, a])
        drain(block_rows(across, us[a], 1), ag2_sem.at[3, a])
    drain(block_rows(across, us[3]), ag2_sem.at[2, 3])
    project(3)
    for kk in range(1, nz):
        drain(part_recv.at[(z + nz - kk) % nz], rs_recv_sem.at[kk - 1])
    for w in range(nx):
        for u in range(ny):
            here = (w * ny + u) * blk
            total = part_own[here : here + blk, :]
            for zz in range(nz):
                total = total + part_recv[zz, here : here + blk, :].astype(F32)
            there = rows_at(block_of(w, u) * blk, blk)
            hid_v[there, :] = total + res_v[there, :]

    hidden = hid_v[...]
    squares = jnp.sum(hidden * hidden, axis=1, keepdims=True)
    high = squares.astype(BF16).astype(F32)
    middle = (squares - high).astype(BF16).astype(F32)
    low = squares - high - middle
    lane = lax.broadcasted_iota(jnp.int32, (tokens, LANES), 1)
    gain = jnp.concatenate([gain_ref[...].astype(F32), jnp.zeros((1, LANES - cols), F32)], axis=1)
    extended = hidden * gain
    extended = jnp.where(lane == cols, high, extended)
    extended = jnp.where(lane == cols + 1, middle, extended)
    extended = jnp.where(lane == cols + 2, low, extended)
    part = cap // 2
    disp[...] = nn_dot(onehot[...], extended.astype(BF16)).astype(BF16).reshape(experts, 2, part, LANES)

    my_slots = rows_at(side * part, part)
    my_lanes = rows_at(own_block * LANES, LANES)
    own_expert = side * plane + own_block
    z_next, z_prev, z_far = (z + 1) % nz, (z + nz - 1) % nz, (z + 2) % nz

    def dispatch_halves(expert, ss, target, dx):
        for h, to in ((0, z_next), (1, z_prev)):
            remote(
                disp.at[expert, h],
                rows.at[z, h, my_slots, my_lanes],
                disp_send_sem.at[1],
                disp_recv_sem.at[1 + h, dx],
                {"side": ss, "dev": target * nz + to},
            ).start()

    def far_first(n):
        return jnp.where(n == 1, 2, jnp.where(n == 2, 1, n))

    def dispatch(i, carry):
        ss = (side + i) % side_n
        sy = (y + far_first((i // side_n) % ny)) % ny
        dx = far_first(i // (side_n * ny))
        target = ((x + dx) % nx) * ny + sy
        expert = ss * plane + target
        dispatch_halves(expert, ss, target, dx)
        remote(
            disp.at[expert],
            rows.at[z, :, my_slots, my_lanes],
            disp_send_sem.at[0],
            disp_recv_sem.at[0, dx],
            {"side": ss, "dev": target * nz + z},
        ).start()
        return carry

    pltpu.make_async_copy(disp.at[own_expert], rows.at[z, :, my_slots, my_lanes], disp_recv_sem.at[0, 0]).start()
    dispatch_halves(own_expert, side, own_block, 0)
    lax.fori_loop(1, experts, dispatch, 0)
    hid_t[...] = hidden.T

    width = ny * LANES
    slots = side_n * cap
    units = wg_v.shape[3]

    def lanes_from(p):
        return pl.ds(pl.multiple_of(p * width, width), width)

    def piece_of(zz, dx, h=None):
        lanes = lanes_from((x + nx - dx) % nx)
        if h is None:
            return rows.at[zz, :, :, lanes]
        return rows.at[zz, h, :, lanes]

    def along(piece, to, n, dx):
        remote(piece, piece, ring_send_sem, ring_recv_sem.at[n], at_ring(to)).start()

    for dx in (0, 2, 1, 3):
        drain(piece_of(z, dx), disp_recv_sem.at[0, dx])
        along(piece_of(z, dx, 1), z_next, 0, dx)
        along(piece_of(z, dx, 0), z_prev, 1, dx)
        drain(piece_of(z_prev, dx, 0), disp_recv_sem.at[1, dx])
        along(piece_of(z_prev, dx, 0), z_next, 2, dx)
        drain(piece_of(z_next, dx, 1), disp_recv_sem.at[2, dx])
        along(piece_of(z_next, dx, 1), z_prev, 3, dx)
    weight_copies[0].wait()
    drain(wg_v.at[:, :, pl.ds(0, cols), :], weight_sem.at[0])
    drain(wu_v.at[:, :, pl.ds(0, cols), :], weight_sem.at[1])
    gate = jnp.zeros((slots, units), F32)
    upward = jnp.zeros((slots, units), F32)
    marks = jnp.zeros((slots, LANES), F32)

    def take(zz, gate, upward, marks):
        lhs = rows[zz].reshape(slots, plane * LANES)
        gate = gate + nn_dot(lhs, wg_v[zz].reshape(plane * LANES, units))
        upward = upward + nn_dot(lhs, wu_v[zz].reshape(plane * LANES, units))
        for j in range(plane):
            marks = marks + lhs[:, j * LANES : (j + 1) * LANES].astype(F32)
        return gate, upward, marks

    gate, upward, marks = take(z, gate, upward, marks)
    drain(rows.at[z_prev, 1], ring_recv_sem.at[0])
    gate, upward, marks = take(z_prev, gate, upward, marks)
    drain(rows.at[z_next, 0], ring_recv_sem.at[1])
    gate, upward, marks = take(z_next, gate, upward, marks)
    drain(rows.at[z_far, 0], ring_recv_sem.at[2])
    drain(rows.at[z_far, 1], ring_recv_sem.at[3])
    gate, upward, marks = take(z_far, gate, upward, marks)
    mark_lane = lax.broadcasted_iota(jnp.int32, (slots, LANES), 1)
    marks = jnp.where((mark_lane >= cols) & (mark_lane < cols + 3), marks, 0.0)
    scale = lax.rsqrt(jnp.sum(marks, axis=1, keepdims=True) / full + NORM_EPS)
    gate = gate * scale
    activated = (gate / (1.0 + jnp.exp(-gate)) * (upward * scale)).astype(BF16)

    group = ny * nz * cols
    turns = (2, 1, 3, 0)
    for k in turns:
        p = (x + k) % nx
        out = nn_dot(activated, wd_v[:, pl.ds(pl.multiple_of(p * group, LANES), group)])
        for a in range(ny):
            for zz in range(nz):
                at = (a * nz + zz) * cols
                piece = jnp.concatenate([out[:, at : at + cols], jnp.zeros((slots, LANES - cols), F32)], axis=1)
                osend[zz, :, :, rows_at((p * ny + a) * LANES, LANES)] = piece.astype(BF16).reshape(
                    2, slots // 2, LANES
                )
        lanes = lanes_from(p)
        for n, (source, h, to) in enumerate(
            ((z_next, 0, z_next), (z_prev, 1, z_prev), (z_far, 0, z_prev), (z_far, 1, z_next))
        ):
            remote(
                osend.at[source, h, :, lanes], near_recv.at[n, :, lanes], near_send_sem, near_recv_sem.at[n, k], at_ring(to)
            ).start()
    for k in turns:
        p = (x + k) % nx
        lanes = lanes_from(p)
        for n, (held, h, place) in enumerate(((z, 0, 0), (z, 1, 1), (z_prev, 0, 2), (z_next, 1, 3))):
            drain(near_recv.at[n, :, lanes], near_recv_sem.at[n, k])
            summed = osend[held, h, :, lanes].astype(F32) + near_recv[n, :, lanes].astype(F32)
            fin[place, :, lanes] = summed.astype(BF16)
        for a in turns:
            target = p * ny + (y + a) % ny
            at = rows_at(target * LANES, LANES)
            for ds in range(side_n):
                ss = (side + ds) % side_n
                its = rows_at(ss * part, part)
                for h, zz in ((0, z_prev), (1, z_next)):
                    remote(
                        fin.at[2 + h, its, at],
                        ret_more.at[own_expert, h],
                        ret_send_sem.at[1],
                        ret_recv_sem.at[1],
                        {"side": ss, "dev": target * nz + zz},
                    ).start()
                src = fin.at[0:2, its, at]
                if k == 0 and a == 0 and ds == 0:
                    pltpu.make_async_copy(src, ret.at[own_expert], ret_recv_sem.at[0]).start()
                else:
                    to = {"side": ss, "dev": target * nz + z}
                    remote(src, ret.at[own_expert], ret_send_sem.at[0], ret_recv_sem.at[0], to).start()

    drain(ret, ret_recv_sem.at[0])
    drain(ret_more, ret_recv_sem.at[1])
    total = (ret[...].astype(F32) + ret_more[...].astype(F32)).reshape(experts * cap, LANES)
    total = (total * wslot[...]).T
    high = total.astype(BF16)
    low = (total - high.astype(F32)).astype(BF16)
    routed = nn_dot(jnp.concatenate([high, low], axis=0), onehot[...])
    result = hid_t[...] + routed[0:LANES] + routed[LANES : 2 * LANES]
    out_v[...] = result[0:cols]
    out_copy = pltpu.make_async_copy(out_v, out_ref, small_sem.at[5])
    out_copy.start()

    drain(wo_v.at[0 : nz - 1, pl.ds(0, cols), my_half], wo_send_sem)
    drain(vu_v.at[0 : (nx - 1) * (ny + 1), my_rows, :], vu_send_sem)
    drain(vu_v.at[:, my_rows, :], vu_swap_send_sem)
    for swap in wo_swaps:
        swap.wait_send()
    drain(ctx_send.at[0 : nz - 1], ctx_send_sem)
    drain(val_v.at[0 : 3 * (ny + 1) * blk], ag_send_sem)
    drain(part_send.at[0 : nz - 1], rs_send_sem)
    drain(disp.at[0 : experts - 1], disp_send_sem.at[0])
    drain(disp, disp_send_sem.at[1])
    drain(ret.at[0 : experts - 1], ret_send_sem.at[0])
    drain(ret_more, ret_send_sem.at[1])
    drain(rows.at[0:2], ring_send_sem)
    drain(near_recv, near_send_sem)
    out_copy.wait()


def per_device(
    queries,
    latent_cache,
    cache_lengths,
    residual,
    value_up,
    out_proj,
    norm_gain,
    expert_ids,
    route_weights,
    w_gate,
    w_up,
    w_down,
):
    side_n = lax.axis_size("side")
    ndev = lax.axis_size("dev")
    nx = 4
    nz = nx
    plane = nx * nx
    tokens, cols = residual.shape
    reqs, heads, width = queries.shape
    length = latent_cache.shape[1]
    latent, vdim = value_up.shape[1:]
    units = w_gate.shape[1]
    experts = side_n * plane
    cap = 32
    blk = nz * reqs
    hbm = pl.BlockSpec(memory_space=pl.ANY)
    dma = pltpu.SemaphoreType.DMA
    out = pl.pallas_call(
        functools.partial(layer_kernel, {"side": side_n, "x": nx, "z": nz}),
        out_shape=jax.ShapeDtypeStruct((cols, tokens), F32),
        in_specs=[hbm] * 12,
        out_specs=hbm,
        scratch_shapes=[
            pltpu.VMEM((reqs, heads, width), BF16),
            pltpu.SMEM((reqs,), jnp.int32),
            pltpu.VMEM((cols, tokens), BF16),
            pltpu.VMEM((1, cols), BF16),
            pltpu.VMEM((expert_ids.shape[1], tokens), jnp.int32),
            pltpu.VMEM((expert_ids.shape[1], tokens), F32),
            pltpu.VMEM((cols, tokens), F32),
            pltpu.VMEM((reqs, width, length), BF16),
            pltpu.VMEM((nz, plane, LANES, units), BF16),
            pltpu.VMEM((nz, plane, LANES, units), BF16),
            pltpu.VMEM((units, ndev * cols), BF16),
            pltpu.VMEM((nz, LANES, plane * LANES), BF16),
            pltpu.VMEM((plane, latent, vdim), BF16),
            pltpu.VMEM((latent // LANES, reqs * heads, LANES), F32),
            pltpu.VMEM((nz, plane * reqs, latent), BF16),
            pltpu.VMEM((nz, plane * reqs, latent), BF16),
            pltpu.VMEM((tokens, plane * LANES), BF16),
            pltpu.VMEM((nz, tokens, LANES), BF16),
            pltpu.VMEM((nz, tokens, LANES), BF16),
            pltpu.VMEM((tokens, LANES), F32),
            pltpu.VMEM((tokens, LANES), F32),
            pltpu.VMEM((tokens, LANES), F32),
            pltpu.VMEM((LANES, tokens), F32),
            pltpu.VMEM((experts, tokens), F32),
            pltpu.VMEM((experts, tokens), F32),
            pltpu.VMEM((experts * cap, tokens), BF16),
            pltpu.VMEM((experts * cap, LANES), F32),
            pltpu.VMEM((experts, 2, cap // 2, LANES), BF16),
            pltpu.VMEM((nz, 2, side_n * cap // 2, plane * LANES), BF16),
            pltpu.VMEM((nz, 2, side_n * cap // 2, plane * LANES), BF16),
            pltpu.VMEM((4, side_n * cap // 2, plane * LANES), BF16),
            pltpu.VMEM((4, side_n * cap // 2, plane * LANES), BF16),
            pltpu.VMEM((experts, 2, cap // 2, LANES), BF16),
            pltpu.VMEM((experts, 2, cap // 2, LANES), BF16),
        ]
        + [
            dma((reqs,)),
            dma(()),
            dma((6,)),
            dma((3,)),
            dma(()),
            dma(()),
            dma((nz - 1, 2)),
            dma(()),
            dma(()),
            dma((nx - 1,)),
            dma((nx - 1,)),
            dma(()),
            dma(()),
            dma((2,)),
            dma((2,)),
            dma(()),
            dma((nz - 1,)),
            dma(()),
            dma((3,)),
            dma((4, nx)),
            dma(()),
            dma((nz - 1,)),
            dma((2,)),
            dma((3, nx)),
            dma(()),
            dma((4,)),
            dma(()),
            dma((4, nx)),
            dma((2,)),
            dma((2,)),
        ],
        compiler_params=pltpu.CompilerParams(
            collective_id=0, has_side_effects=True, vmem_limit_bytes=56 * 1024 * 1024
        ),
    )(
        queries,
        latent_cache.transpose(0, 2, 1),
        cache_lengths,
        residual.T,
        value_up,
        out_proj.T,
        norm_gain.reshape(1, cols),
        expert_ids.T,
        route_weights.T,
        w_gate.reshape(plane, nz, cols, units),
        w_up.reshape(plane, nz, cols, units),
        w_down,
    )
    return out.astype(BF16).T


def solution(mesh):
    placed = (
        P(("side", "dev"), None, None),
        P(("side", "dev"), None, None),
        P(("side", "dev")),
        P("side", "dev"),
        P("dev", None, None),
        P(None, "dev"),
        P("dev"),
        P("side", None),
        P("side", None),
        P(None, ("side", "dev")),
        P(None, ("side", "dev")),
        P(("side", "dev"), None),
    )
    return jax.shard_map(
        per_device, mesh=mesh, in_specs=placed, out_specs=P("side", "dev"), check_vma=False
    )
```

```python
import functools

import jax
import jax.numpy as jnp
from jax import lax
from jax.experimental import pallas as pl
from jax.experimental.pallas import tpu as pltpu
from jax.sharding import PartitionSpec as P

MESH = pl.DeviceIdType.MESH
LANES = 128
SCORE_SCALE = 192.0 ** (-0.5)
NORM_EPS = 1e-06
BF16 = jnp.bfloat16
F32 = jnp.float32


def nt_dot(a, b):
    return lax.dot_general(a, b, (((1,), (1,)), ((), ())), preferred_element_type=F32)


def nn_dot(a, b):
    return jnp.dot(a, b, preferred_element_type=F32)


def layer_kernel(
    dims,
    q_hbm,
    cache_ref,
    len_hbm,
    res_hbm,
    vu_ref,
    wo_ref,
    gain_hbm,
    ids_hbm,
    rw_hbm,
    wg_ref,
    wu_ref,
    wd_ref,
    out_ref,
    q_ref,
    len_ref,
    res_ref,
    gain_ref,
    ids_ref,
    rw_ref,
    out_v,
    cache_v,
    wg_v,
    wu_v,
    wd_v,
    wo_v,
    vu_v,
    ctx_f,
    ctx_send,
    ctx_recv,
    val_v,
    part_send,
    part_recv,
    part_own,
    res_v,
    hid_v,
    hid_t,
    pos_v,
    wte_v,
    onehot,
    wslot,
    disp,
    rows,
    osend,
    near_recv,
    fin,
    ret,
    ret_more,
    cache_sem,
    q_sem,
    small_sem,
    weight_sem,
    wo_sem,
    wo_send_sem,
    wo_recv_sem,
    vu_sem,
    vu_send_sem,
    vu1_sem,
    vu2_sem,
    vu_swap_send_sem,
    vu_swap_recv_sem,
    wo_swap_send_sem,
    wo_swap_recv_sem,
    ctx_send_sem,
    ctx_recv_sem,
    ag_send_sem,
    ag1_sem,
    ag2_sem,
    rs_send_sem,
    rs_recv_sem,
    disp_send_sem,
    disp_recv_sem,
    ring_send_sem,
    ring_recv_sem,
    near_send_sem,
    near_recv_sem,
    ret_send_sem,
    ret_recv_sem,
):
    side_n, nx, nz = dims["side"], dims["x"], dims["z"]
    ny = nx
    plane = nx * ny
    ndev = plane * nz
    reqs, heads, _ = q_ref.shape
    length = cache_ref.shape[2]
    latent = vu_ref.shape[1]
    vdim = vu_ref.shape[2]
    cols = res_ref.shape[0]
    tokens = res_ref.shape[1]
    blk = nz * reqs
    chunk = ny * blk
    half = plane // side_n
    experts = side_n * plane
    cap = onehot.shape[0] // experts
    full = ndev * cols
    side = lax.axis_index("side")
    dev = lax.axis_index("dev")
    x = dev // (ny * nz)
    y = (dev // nz) % ny
    z = dev % nz
    own_block = x * ny + y
    up = jnp.where(side == 0, x, y)
    uq = jnp.where(side == 0, y, x)
    twin = 1 - side

    def block_of(w, u):
        return jnp.where(side == 0, w * ny + u, u * ny + w)

    def at_plane(block):
        return {"side": side, "dev": block * nz + z}

    def at_ring(zz):
        return {"side": side, "dev": own_block * nz + zz}

    def remote(src, dst, send, recv, target):
        return pltpu.make_async_remote_copy(
            src_ref=src, dst_ref=dst, send_sem=send, recv_sem=recv, device_id=target, device_id_type=MESH
        )

    def drain(ref, sem):
        pltpu.make_async_copy(ref, ref, sem).wait()

    def rows_at(start, size):
        return pl.ds(pl.multiple_of(start, size), size)

    for zz in range(nz):
        wo_v[zz, cols:, :] = jnp.zeros((LANES - cols, plane * LANES), BF16)
    barrier = pltpu.get_barrier_semaphore()
    mate = {"side": twin, "dev": dev}
    friends = [mate]
    for k in range(1, nx):
        friends.append({"side": side, "dev": (((x + k) % nx) * ny + y) * nz + z})
        friends.append({"side": side, "dev": (x * ny + (y + k) % ny) * nz + z})
        friends.append({"side": side, "dev": own_block * nz + (z + k) % nz})
    for friend in friends:
        pl.semaphore_signal(barrier, inc=1, device_id=friend, device_id_type=MESH)

    half_lanes = half * LANES
    half_rows = latent // side_n
    my_half = pl.ds(pl.multiple_of(side * half_lanes, half_lanes), half_lanes)
    my_rows = rows_at(side * half_rows, half_rows)

    def wo_source(j, zz):
        return wo_ref.at[:, rows_at((j * nz + zz) * LANES, LANES)]

    def wo_place(zz, j):
        return wo_v.at[zz, pl.ds(0, cols), rows_at(j * LANES, LANES)]

    own_vu = pltpu.make_async_copy(vu_ref.at[0, my_rows, :], vu_v.at[own_block, my_rows, :], vu_sem)
    own_vu.start()
    len_copy = pltpu.make_async_copy(len_hbm, len_ref, small_sem.at[0])
    len_copy.start()
    q_copy = pltpu.make_async_copy(q_hbm, q_ref, q_sem)
    q_copy.start()
    for r in range(2):
        pltpu.make_async_copy(cache_ref.at[r], cache_v.at[r], cache_sem.at[r]).start()
    small_copies = [
        pltpu.make_async_copy(source, place, small_sem.at[n + 1])
        for n, (source, place) in enumerate(
            ((res_hbm, res_ref), (gain_hbm, gain_ref), (ids_hbm, ids_ref), (rw_hbm, rw_ref))
        )
    ]
    weight_copies = [pltpu.make_async_copy(wd_ref, wd_v, weight_sem.at[2])]
    for zz in range(nz):
        for n, (source, place) in enumerate(((wg_ref, wg_v), (wu_ref, wu_v))):
            weight_copies.append(
                pltpu.make_async_copy(source.at[:, zz], place.at[zz, :, pl.ds(0, cols), :], weight_sem.at[n])
            )

    place_no = lax.broadcasted_iota(jnp.int32, (1, length), 1)

    def attend(first):
        pair = (first, first + 1)
        for r in pair:
            pltpu.make_async_copy(cache_ref.at[r], cache_v.at[r], cache_sem.at[r]).wait()
        if first == 0:
            for r in range(2, reqs):
                pltpu.make_async_copy(cache_ref.at[r], cache_v.at[r], cache_sem.at[r]).start()
        scores = []
        for r in pair:
            outside = jnp.where(place_no < len_ref[r], 0.0, -1e30)
            scores.append(nn_dot(q_ref[r], cache_v[r]) * SCORE_SCALE + outside)
        for r, own in zip(pair, scores):
            weights = jnp.exp(own - jnp.max(own, axis=1, keepdims=True))
            weights = (weights * (1.0 / jnp.sum(weights, axis=1, keepdims=True))).astype(BF16)
            context = nt_dot(weights, cache_v[r, 0:latent, :])
            for b in range(latent // LANES):
                ctx_f[b, r * heads : (r + 1) * heads, :] = context[:, b * LANES : (b + 1) * LANES]

    pl.semaphore_wait(barrier, len(friends))
    for k in (1, 3, 2):
        remote(
            vu_ref.at[0, my_rows, :],
            vu_v.at[own_block, my_rows, :],
            vu_send_sem,
            vu1_sem.at[k - 1],
            at_plane(block_of(up, (uq + k) % ny)),
        ).start()
    cuts = (0, half // 4, half)

    def lanes_of(part):
        start = side * half_lanes + cuts[part] * LANES
        return pl.ds(pl.multiple_of(start, LANES), (cuts[part + 1] - cuts[part]) * LANES)

    def exchange_wo(part):
        for i in range(cuts[part], cuts[part + 1]):
            for k in range(1, nz):
                to = (z + k) % nz
                j = side * half + i
                remote(
                    wo_source(j, to), wo_place(z, j), wo_send_sem, wo_recv_sem.at[k - 1, part], at_ring(to)
                ).start()

    def swap_wo(part):
        for k in range(1, nz):
            drain(wo_v.at[(z + nz - k) % nz, pl.ds(0, cols), lanes_of(part)], wo_recv_sem.at[k - 1, part])
        piece = wo_v.at[:, :, lanes_of(part)]
        copy = remote(piece, piece, wo_swap_send_sem.at[part], wo_swap_recv_sem.at[part], mate)
        copy.start()
        return copy

    def forward_vu(a):
        block = block_of(up, (uq + ny - a) % ny)
        piece = vu_v.at[block, my_rows, :]
        if a > 0:
            drain(piece, vu1_sem.at[a - 1])
        for k in (1, 3, 2):
            to = at_plane(block_of((up + k) % nx, uq))
            source = piece if a > 0 else vu_ref.at[0, my_rows, :]
            remote(source, piece, vu_send_sem, vu2_sem.at[k - 1], to).start()

    exchange_wo(0)
    len_copy.wait()
    q_copy.wait()

    pairs = reqs // 2

    def send_contexts(g):
        for r in (2 * g, 2 * g + 1):
            for zz in range(nz):
                pieces = [
                    ctx_f[b, pl.ds(r * heads + zz, plane, stride=nz), :] for b in range(latent // LANES)
                ]
                ctx_send[zz, r * plane : (r + 1) * plane, :] = jnp.concatenate(pieces, axis=1).astype(BF16)
        at = pl.ds(2 * g * plane, 2 * plane)
        for k in (2, 1, 3):
            to = (z + k) % nz
            remote(
                ctx_send.at[to, at, :], ctx_recv.at[z, at, :], ctx_send_sem, ctx_recv_sem.at[k - 1], at_ring(to)
            ).start()

    for g in range(pairs):
        attend(2 * g)
        send_contexts(g)
        if g == 0:
            forward_vu(0)
            for i in range(half):
                j = side * half + i
                pltpu.make_async_copy(wo_source(j, z), wo_place(z, j), wo_sem).start()
        if g == 1:
            forward_vu(1)
            forward_vu(3)
        if g == 2:
            forward_vu(2)
            for copy in small_copies + weight_copies:
                copy.start()
    exchange_wo(1)
    ctx_recv[z] = ctx_send[z]

    def swap_vu(k):
        w = (up + nx - k) % nx
        if k == 0:
            own_vu.wait()
        else:
            drain(vu_v.at[0:ny, my_rows, :], vu2_sem.at[k - 1])
        for a in range(ny):
            block = block_of(w, (uq + ny - a) % ny)
            piece = vu_v.at[block, my_rows, :]
            remote(piece, piece, vu_swap_send_sem, vu_swap_recv_sem, mate).start()

    for k in (0, 1, 3, 2):
        swap_vu(k)
    drain(wo_v.at[z, pl.ds(0, cols), my_half], wo_sem)
    wo_swaps = [swap_wo(0)]

    for copy in small_copies:
        copy.wait()
    ids = ids_ref[...]
    rw = rw_ref[...]
    expert_no = lax.broadcasted_iota(jnp.int32, (experts, tokens), 0)
    chosen = jnp.zeros((experts, tokens), F32)
    wte = jnp.zeros((experts, tokens), F32)
    for k in range(ids.shape[0]):
        match = ids[k : k + 1, :] == expert_no
        chosen = jnp.where(match, 1.0, chosen)
        wte = wte + jnp.where(match, rw[k : k + 1, :], 0.0)
    before = lax.broadcasted_iota(jnp.int32, (tokens, tokens), 0) < lax.broadcasted_iota(
        jnp.int32, (tokens, tokens), 1
    )
    position = nn_dot(chosen.astype(BF16), jnp.where(before, 1.0, 0.0).astype(BF16))
    pos_v[...] = jnp.where(chosen > 0.0, position, -1.0)
    wte_v[...] = wte

    def fill(e, carry):
        slot = lax.broadcasted_iota(jnp.int32, (cap, tokens), 0).astype(F32)
        hit = pos_v[pl.ds(e, 1), :] == slot
        onehot[rows_at(e * cap, cap), :] = jnp.where(hit, 1.0, 0.0).astype(BF16)
        picked = jnp.sum(jnp.where(hit, wte_v[pl.ds(e, 1), :], 0.0), axis=1, keepdims=True)
        wslot[rows_at(e * cap, cap), :] = jnp.broadcast_to(picked, (cap, LANES))
        return carry

    res_t = jnp.concatenate(
        [res_ref[...].astype(F32), jnp.zeros((LANES - cols, tokens), F32)], axis=0
    )
    res_v[...] = res_t.T
    for zz in range(nz):
        for j in range(plane):
            wg_v[zz, j, cols:, :] = jnp.zeros((LANES - cols, wg_v.shape[3]), BF16)
            wu_v[zz, j, cols:, :] = jnp.zeros((LANES - cols, wu_v.shape[3]), BF16)
    part_recv[z] = jnp.zeros((tokens, LANES), BF16)

    lax.fori_loop(0, experts // 4, fill, 0)
    drain(vu_v.at[:, rows_at(twin * half_rows, half_rows), :], vu_swap_recv_sem)
    for k in range(1, nz):
        drain(ctx_recv.at[(z + nz - k) % nz], ctx_recv_sem.at[k - 1])
    my_block = rows_at(own_block * blk, blk)
    for zz in range(nz):
        for b in range(latent // LANES):
            ctx_f[b, zz * reqs * plane : (zz + 1) * reqs * plane, :] = ctx_recv[
                zz, :, b * LANES : (b + 1) * LANES
            ].astype(F32)
    for jp in range(plane // 2):
        lhs = [
            jnp.concatenate(
                [ctx_f[b, pl.ds(j, blk, stride=plane), :] for b in range(latent // LANES)], axis=1
            )
            for j in (2 * jp, 2 * jp + 1)
        ]
        rhs = jnp.concatenate([vu_v[2 * jp], vu_v[2 * jp + 1]], axis=1)
        both = nn_dot(jnp.concatenate(lhs, axis=0).astype(BF16), rhs)
        picked = jnp.concatenate([both[0:blk, 0:vdim], both[blk : 2 * blk, vdim : 2 * vdim]], axis=1)
        val_v[my_block, jp * 2 * vdim : (jp + 1) * 2 * vdim] = picked.astype(BF16)

    half_blk = blk // 2

    def block_rows(w, u, part=None):
        start = block_of(w, u) * blk
        if part is None:
            return val_v.at[rows_at(start, blk), :]
        return val_v.at[rows_at(start + part * half_blk, half_blk), :]

    ahead, behind = (up + 1) % nx, (up + nx - 1) % nx
    across = (up + 2) % nx
    u_ahead, u_behind, u_across = (uq + 1) % ny, (uq + ny - 1) % ny, (uq + 2) % ny

    def pass_u(piece, u, sem):
        remote(piece, piece, ag_send_sem, ag1_sem.at[sem], at_plane(block_of(up, u))).start()

    def pass_w(piece, forward, sem, a):
        to = at_plane(block_of(ahead if forward else behind, uq))
        remote(piece, piece, ag_send_sem, ag2_sem.at[sem, a], to).start()

    us = [uq, u_behind, u_ahead, u_across]
    mine = block_rows(up, uq)
    pass_u(mine, u_ahead, 0)
    pass_u(mine, u_behind, 1)
    lax.fori_loop(experts // 4, experts // 2, fill, 0)
    pass_u(mine, u_across, 2)
    lax.fori_loop(experts // 2, experts, fill, 0)
    pass_w(mine, True, 0, 0)
    pass_w(mine, False, 1, 0)
    for a in range(1, ny):
        piece = block_rows(up, us[a])
        drain(piece, ag1_sem.at[a - 1])
        pass_w(piece, True, 0, a)
        pass_w(piece, False, 1, a)
        if a == 2:
            wo_swaps.append(swap_wo(1))
        if a == 3:
            to = at_plane(block_of(across, uq))
            remote(piece, piece, ag_send_sem, ag2_sem.at[2, a], to).start()

    def hand_on(a):
        drain(block_rows(behind, us[a]), ag2_sem.at[0, a])
        pass_w(block_rows(behind, us[a], 0), True, 2, a)
        drain(block_rows(ahead, us[a]), ag2_sem.at[1, a])
        pass_w(block_rows(ahead, us[a], 1), False, 3, a)

    def project(k):
        w = (up, behind, ahead, across)[k]
        lhs = jnp.concatenate([val_v[rows_at(block_of(w, u) * blk, blk), :] for u in range(ny)], axis=0)
        at = rows_at(w * chunk, chunk)
        own = jnp.zeros((chunk, LANES), F32)
        for zz in range(nz):
            part = nt_dot(lhs, wo_v[zz])
            own = jnp.where(z == zz, part, own)
            part_send[zz, at, :] = part.astype(BF16)
        part_own[at, :] = own
        for kk in (2, 1, 3):
            to = (z + kk) % nz
            remote(
                part_send.at[to, at, :], part_recv.at[z, at, :], rs_send_sem, rs_recv_sem.at[kk - 1], at_ring(to)
            ).start()

    hand_on(0)
    for swap in wo_swaps:
        swap.wait_recv()
    project(0)
    hand_on(1)
    hand_on(2)
    for sem, w in ((0, behind), (1, ahead)):
        drain(block_rows(w, us[3]), ag2_sem.at[sem, 3])
    project(1)
    project(2)
    for a in range(ny - 1):
        drain(block_rows(across, us[a], 0), ag2_sem.at[2, a])
        drain(block_rows(across, us[a], 1), ag2_sem.at[3, a])
    drain(block_rows(across, us[3]), ag2_sem.at[2, 3])
    project(3)
    for kk in range(1, nz):
        drain(part_recv.at[(z + nz - kk) % nz], rs_recv_sem.at[kk - 1])
    for w in range(nx):
        for u in range(ny):
            here = (w * ny + u) * blk
            total = part_own[here : here + blk, :]
            for zz in range(nz):
                total = total + part_recv[zz, here : here + blk, :].astype(F32)
            there = rows_at(block_of(w, u) * blk, blk)
            hid_v[there, :] = total + res_v[there, :]

    hidden = hid_v[...]
    squares = jnp.sum(hidden * hidden, axis=1, keepdims=True)
    high = squares.astype(BF16).astype(F32)
    middle = (squares - high).astype(BF16).astype(F32)
    low = squares - high - middle
    lane = lax.broadcasted_iota(jnp.int32, (tokens, LANES), 1)
    gain = jnp.concatenate([gain_ref[...].astype(F32), jnp.zeros((1, LANES - cols), F32)], axis=1)
    extended = hidden * gain
    extended = jnp.where(lane == cols, high, extended)
    extended = jnp.where(lane == cols + 1, middle, extended)
    extended = jnp.where(lane == cols + 2, low, extended)
    part = cap // 2
    extended = extended.astype(BF16)

    my_slots = rows_at(side * part, part)
    my_lanes = rows_at(own_block * LANES, LANES)
    own_expert = side * plane + own_block
    z_next, z_prev, z_far = (z + 1) % nz, (z + nz - 1) % nz, (z + 2) % nz

    def dispatch_halves(expert, ss, target, dx):
        for h, to in ((0, z_next), (1, z_prev)):
            remote(
                disp.at[expert, h],
                rows.at[z, h, my_slots, my_lanes],
                disp_send_sem.at[1],
                disp_recv_sem.at[1 + h, dx],
                {"side": ss, "dev": target * nz + to},
            ).start()

    def far_first(n):
        return jnp.where(n == 1, 2, jnp.where(n == 2, 1, n))

    def dispatch(i, carry):
        ss = (side + i) % side_n
        sy = (y + far_first((i // side_n) % ny)) % ny
        dx = far_first(i // (side_n * ny))
        target = ((x + dx) % nx) * ny + sy
        expert = ss * plane + target
        dispatch_halves(expert, ss, target, dx)
        remote(
            disp.at[expert],
            rows.at[z, :, my_slots, my_lanes],
            disp_send_sem.at[0],
            disp_recv_sem.at[0, dx],
            {"side": ss, "dev": target * nz + z},
        ).start()
        return carry

    for turn in range(nx):
        column = (x + (0, 2, 1, 3)[turn]) % nx
        for ss in range(side_n):
            first = ss * plane + column * ny
            picked = nn_dot(onehot[rows_at(first * cap, ny * cap), :], extended)
            disp[pl.ds(first, ny)] = picked.astype(BF16).reshape(ny, 2, part, LANES)
        if turn == 0:
            pltpu.make_async_copy(
                disp.at[own_expert], rows.at[z, :, my_slots, my_lanes], disp_recv_sem.at[0, 0]
            ).start()
            dispatch_halves(own_expert, side, own_block, 0)
        per_turn = side_n * ny
        lax.fori_loop(max(1, turn * per_turn), (turn + 1) * per_turn, dispatch, 0)
    hid_t[...] = hidden.T

    width = ny * LANES
    slots = side_n * cap
    units = wg_v.shape[3]

    def lanes_from(p):
        return pl.ds(pl.multiple_of(p * width, width), width)

    def piece_of(zz, dx, h=None):
        lanes = lanes_from((x + nx - dx) % nx)
        if h is None:
            return rows.at[zz, :, :, lanes]
        return rows.at[zz, h, :, lanes]

    def along(piece, to, n, dx):
        remote(piece, piece, ring_send_sem, ring_recv_sem.at[n], at_ring(to)).start()

    for dx in (0, 2, 1, 3):
        drain(piece_of(z, dx), disp_recv_sem.at[0, dx])
        along(piece_of(z, dx, 1), z_next, 0, dx)
        along(piece_of(z, dx, 0), z_prev, 1, dx)
        drain(piece_of(z_prev, dx, 0), disp_recv_sem.at[1, dx])
        along(piece_of(z_prev, dx, 0), z_next, 2, dx)
        drain(piece_of(z_next, dx, 1), disp_recv_sem.at[2, dx])
        along(piece_of(z_next, dx, 1), z_prev, 3, dx)
    weight_copies[0].wait()
    drain(wg_v.at[:, :, pl.ds(0, cols), :], weight_sem.at[0])
    drain(wu_v.at[:, :, pl.ds(0, cols), :], weight_sem.at[1])
    gate = jnp.zeros((slots, units), F32)
    upward = jnp.zeros((slots, units), F32)
    marks = jnp.zeros((slots, LANES), F32)

    def take(zz, gate, upward, marks):
        lhs = rows[zz].reshape(slots, plane * LANES)
        gate = gate + nn_dot(lhs, wg_v[zz].reshape(plane * LANES, units))
        upward = upward + nn_dot(lhs, wu_v[zz].reshape(plane * LANES, units))
        for j in range(plane):
            marks = marks + lhs[:, j * LANES : (j + 1) * LANES].astype(F32)
        return gate, upward, marks

    gate, upward, marks = take(z, gate, upward, marks)
    drain(rows.at[z_prev, 1], ring_recv_sem.at[0])
    gate, upward, marks = take(z_prev, gate, upward, marks)
    drain(rows.at[z_next, 0], ring_recv_sem.at[1])
    gate, upward, marks = take(z_next, gate, upward, marks)
    drain(rows.at[z_far, 0], ring_recv_sem.at[2])
    drain(rows.at[z_far, 1], ring_recv_sem.at[3])
    gate, upward, marks = take(z_far, gate, upward, marks)
    mark_lane = lax.broadcasted_iota(jnp.int32, (slots, LANES), 1)
    marks = jnp.where((mark_lane >= cols) & (mark_lane < cols + 3), marks, 0.0)
    scale = lax.rsqrt(jnp.sum(marks, axis=1, keepdims=True) / full + NORM_EPS)
    gate = gate * scale
    activated = (gate / (1.0 + jnp.exp(-gate)) * (upward * scale)).astype(BF16)

    group = ny * nz * cols
    turns = (2, 1, 3, 0)
    for k in turns:
        p = (x + k) % nx
        out = nn_dot(activated, wd_v[:, pl.ds(pl.multiple_of(p * group, LANES), group)])
        for a in range(ny):
            for zz in range(nz):
                at = (a * nz + zz) * cols
                piece = jnp.concatenate([out[:, at : at + cols], jnp.zeros((slots, LANES - cols), F32)], axis=1)
                osend[zz, :, :, rows_at((p * ny + a) * LANES, LANES)] = piece.astype(BF16).reshape(
                    2, slots // 2, LANES
                )
        lanes = lanes_from(p)
        for n, (source, h, to) in enumerate(
            ((z_next, 0, z_next), (z_prev, 1, z_prev), (z_far, 0, z_prev), (z_far, 1, z_next))
        ):
            remote(
                osend.at[source, h, :, lanes], near_recv.at[n, :, lanes], near_send_sem, near_recv_sem.at[n, k], at_ring(to)
            ).start()
    for k in turns:
        p = (x + k) % nx
        lanes = lanes_from(p)
        for n, (held, h, place) in enumerate(((z, 0, 0), (z, 1, 1), (z_prev, 0, 2), (z_next, 1, 3))):
            drain(near_recv.at[n, :, lanes], near_recv_sem.at[n, k])
            summed = osend[held, h, :, lanes].astype(F32) + near_recv[n, :, lanes].astype(F32)
            fin[place, :, lanes] = summed.astype(BF16)
        for a in turns:
            target = p * ny + (y + a) % ny
            at = rows_at(target * LANES, LANES)
            for ds in range(side_n):
                ss = (side + ds) % side_n
                its = rows_at(ss * part, part)
                for h, zz in ((0, z_prev), (1, z_next)):
                    remote(
                        fin.at[2 + h, its, at],
                        ret_more.at[own_expert, h],
                        ret_send_sem.at[1],
                        ret_recv_sem.at[1],
                        {"side": ss, "dev": target * nz + zz},
                    ).start()
                src = fin.at[0:2, its, at]
                if k == 0 and a == 0 and ds == 0:
                    pltpu.make_async_copy(src, ret.at[own_expert], ret_recv_sem.at[0]).start()
                else:
                    to = {"side": ss, "dev": target * nz + z}
                    remote(src, ret.at[own_expert], ret_send_sem.at[0], ret_recv_sem.at[0], to).start()

    drain(ret, ret_recv_sem.at[0])
    drain(ret_more, ret_recv_sem.at[1])
    total = (ret[...].astype(F32) + ret_more[...].astype(F32)).reshape(experts * cap, LANES)
    total = (total * wslot[...]).T
    high = total.astype(BF16)
    low = (total - high.astype(F32)).astype(BF16)
    routed = nn_dot(jnp.concatenate([high, low], axis=0), onehot[...])
    result = hid_t[...] + routed[0:LANES] + routed[LANES : 2 * LANES]
    out_v[...] = result[0:cols]
    out_copy = pltpu.make_async_copy(out_v, out_ref, small_sem.at[5])
    out_copy.start()

    drain(wo_v.at[0 : nz - 1, pl.ds(0, cols), my_half], wo_send_sem)
    drain(vu_v.at[0 : (nx - 1) * (ny + 1), my_rows, :], vu_send_sem)
    drain(vu_v.at[:, my_rows, :], vu_swap_send_sem)
    for swap in wo_swaps:
        swap.wait_send()
    drain(ctx_send.at[0 : nz - 1], ctx_send_sem)
    drain(val_v.at[0 : 3 * (ny + 1) * blk], ag_send_sem)
    drain(part_send.at[0 : nz - 1], rs_send_sem)
    drain(disp.at[0 : experts - 1], disp_send_sem.at[0])
    drain(disp, disp_send_sem.at[1])
    drain(ret.at[0 : experts - 1], ret_send_sem.at[0])
    drain(ret_more, ret_send_sem.at[1])
    drain(rows.at[0:2], ring_send_sem)
    drain(near_recv, near_send_sem)
    out_copy.wait()


def per_device(
    queries,
    latent_cache,
    cache_lengths,
    residual,
    value_up,
    out_proj,
    norm_gain,
    expert_ids,
    route_weights,
    w_gate,
    w_up,
    w_down,
):
    side_n = lax.axis_size("side")
    ndev = lax.axis_size("dev")
    nx = 4
    nz = nx
    plane = nx * nx
    tokens, cols = residual.shape
    reqs, heads, width = queries.shape
    length = latent_cache.shape[1]
    latent, vdim = value_up.shape[1:]
    units = w_gate.shape[1]
    experts = side_n * plane
    cap = 32
    blk = nz * reqs
    hbm = pl.BlockSpec(memory_space=pl.ANY)
    dma = pltpu.SemaphoreType.DMA
    out = pl.pallas_call(
        functools.partial(layer_kernel, {"side": side_n, "x": nx, "z": nz}),
        out_shape=jax.ShapeDtypeStruct((cols, tokens), F32),
        in_specs=[hbm] * 12,
        out_specs=hbm,
        scratch_shapes=[
            pltpu.VMEM((reqs, heads, width), BF16),
            pltpu.SMEM((reqs,), jnp.int32),
            pltpu.VMEM((cols, tokens), BF16),
            pltpu.VMEM((1, cols), BF16),
            pltpu.VMEM((expert_ids.shape[1], tokens), jnp.int32),
            pltpu.VMEM((expert_ids.shape[1], tokens), F32),
            pltpu.VMEM((cols, tokens), F32),
            pltpu.VMEM((reqs, width, length), BF16),
            pltpu.VMEM((nz, plane, LANES, units), BF16),
            pltpu.VMEM((nz, plane, LANES, units), BF16),
            pltpu.VMEM((units, ndev * cols), BF16),
            pltpu.VMEM((nz, LANES, plane * LANES), BF16),
            pltpu.VMEM((plane, latent, vdim), BF16),
            pltpu.VMEM((latent // LANES, reqs * heads, LANES), F32),
            pltpu.VMEM((nz, plane * reqs, latent), BF16),
            pltpu.VMEM((nz, plane * reqs, latent), BF16),
            pltpu.VMEM((tokens, plane * LANES), BF16),
            pltpu.VMEM((nz, tokens, LANES), BF16),
            pltpu.VMEM((nz, tokens, LANES), BF16),
            pltpu.VMEM((tokens, LANES), F32),
            pltpu.VMEM((tokens, LANES), F32),
            pltpu.VMEM((tokens, LANES), F32),
            pltpu.VMEM((LANES, tokens), F32),
            pltpu.VMEM((experts, tokens), F32),
            pltpu.VMEM((experts, tokens), F32),
            pltpu.VMEM((experts * cap, tokens), BF16),
            pltpu.VMEM((experts * cap, LANES), F32),
            pltpu.VMEM((experts, 2, cap // 2, LANES), BF16),
            pltpu.VMEM((nz, 2, side_n * cap // 2, plane * LANES), BF16),
            pltpu.VMEM((nz, 2, side_n * cap // 2, plane * LANES), BF16),
            pltpu.VMEM((4, side_n * cap // 2, plane * LANES), BF16),
            pltpu.VMEM((4, side_n * cap // 2, plane * LANES), BF16),
            pltpu.VMEM((experts, 2, cap // 2, LANES), BF16),
            pltpu.VMEM((experts, 2, cap // 2, LANES), BF16),
        ]
        + [
            dma((reqs,)),
            dma(()),
            dma((6,)),
            dma((3,)),
            dma(()),
            dma(()),
            dma((nz - 1, 2)),
            dma(()),
            dma(()),
            dma((nx - 1,)),
            dma((nx - 1,)),
            dma(()),
            dma(()),
            dma((2,)),
            dma((2,)),
            dma(()),
            dma((nz - 1,)),
            dma(()),
            dma((3,)),
            dma((4, nx)),
            dma(()),
            dma((nz - 1,)),
            dma((2,)),
            dma((3, nx)),
            dma(()),
            dma((4,)),
            dma(()),
            dma((4, nx)),
            dma((2,)),
            dma((2,)),
        ],
        compiler_params=pltpu.CompilerParams(
            collective_id=0, has_side_effects=True, vmem_limit_bytes=56 * 1024 * 1024
        ),
    )(
        queries,
        latent_cache.transpose(0, 2, 1),
        cache_lengths,
        residual.T,
        value_up,
        out_proj.T,
        norm_gain.reshape(1, cols),
        expert_ids.T,
        route_weights.T,
        w_gate.reshape(plane, nz, cols, units),
        w_up.reshape(plane, nz, cols, units),
        w_down,
    )
    return out.astype(BF16).T


def solution(mesh):
    placed = (
        P(("side", "dev"), None, None),
        P(("side", "dev"), None, None),
        P(("side", "dev")),
        P("side", "dev"),
        P("dev", None, None),
        P(None, "dev"),
        P("dev"),
        P("side", None),
        P("side", None),
        P(None, ("side", "dev")),
        P(None, ("side", "dev")),
        P(("side", "dev"), None),
    )
    return jax.shard_map(
        per_device, mesh=mesh, in_specs=placed, out_specs=P("side", "dev"), check_vma=False
    )
```
